128 devices in a mesh: bx: 16 (over y_lo, z, core), by: 8 (over y_hi, x).
Axes of the slice: x: 4, y: 4 (y_hi: 2, y_lo: 2; y = y_hi * 2 + y_lo), z: 4, core: 2. Of those that a mesh axis runs over, the one named last changes fastest.
Arguments:
- weights: float32 [16, 8, 2, 64, 8192], P('bx', 'by'), may hold values from -6 to 6
- phase_slope: float32 [8, 16, 8, 8192], P(None, 'bx', 'by'), may hold values from -3.140625 to 3.140625
- interp_matrix: float32 [2, 2, 2, 64, 2, 64], replicated, may hold values from -0.375 to 0.375
- evaluation: float32 [2, 64, 64], replicated, may hold values from -0.5 to 0.5
Outputs:
- target_field: float32 [16, 8, 64, 8192], P('bx', 'by')
The draws below stay inside these ranges and needn't reach their ends.
All inputs are finite; a program needn't handle non-finite values.
Results may differ from the reference program's by a relative error of at most 0.00011.
Values sent between devices are 32-bit elements; how exact they have to be, the bound alone decides.
No kernel may reach another device: no remote copies, remote signals or barrier semaphores. Data moves between devices by JAX's collectives and lax.ppermute only.
A program may use at most 128 MiB of HBM per device.

```python
import jax
import jax.numpy as jnp
import numpy as np
from jax import lax

CHEB = 8
R2 = 64
SLOTS = 8192
LEVELS = 4
STEPS = 8
GX = 16
GY = 8


def shard_levels(stream_key, dims, split, smallest, largest):
    gain = 1.0
    for axis_at, blocks in split:
        heights = jax.random.uniform(jax.random.fold_in(jax.random.fold_in(stream_key, 6), axis_at), (blocks,), jnp.float32, smallest / len(split), largest / len(split))
        gain = gain * jnp.repeat(jnp.exp(heights), dims[axis_at] // blocks).reshape((-1,) + (1,) * (len(dims) - 1 - axis_at))
    return gain


def scatter_about(key, extent, deviation, limit, shards=(), held_as=jnp.bfloat16):
    result = jax.random.normal(key, extent, jnp.float32) * deviation
    if len(shards) > 0:
        result = shard_levels(key, extent, shards, -0.22, 0.18) * result
    return jnp.clip(result, min=-limit, max=limit).astype(held_as)


def setup_inputs(seed: int = 0) -> dict:
    arg_keys = jax.random.split(jax.random.key(seed), 5)
    return {
        "weights": scatter_about(arg_keys[0], (GX, GY, 2, R2, SLOTS), 1.0, 6.0, ((0, 16), (1, 8)), jnp.float32),
        "phase_slope": jnp.clip(jax.random.uniform(arg_keys[1], (STEPS, GX, GY, SLOTS), jnp.float32, -3.140625, 3.140625), -3.140625, 3.140625),
        "interp_matrix": scatter_about(arg_keys[2], (2, 2, 2, R2, 2, R2), (4 * R2) ** -0.5, 0.375, (), jnp.float32),
        "evaluation": scatter_about(arg_keys[3], (2, R2, R2), (2 * R2) ** -0.5, 0.5, (), jnp.float32),
    }


def cheb_nodes(direction):
    points = jnp.cos(jnp.pi * (2.0 * jnp.arange(CHEB, dtype=jnp.float32) + 1.0) / (2.0 * CHEB))
    return jnp.repeat(points, CHEB) if direction == 0 else jnp.tile(points, CHEB)


def merge_global(current, which_axis, bit_no, interp_dir, angles, node_values):
    count = current.shape[which_axis]
    index_all = np.arange(count)
    lower_index = jnp.asarray(index_all & ~(1 << bit_no), dtype=jnp.int32)
    upper_index = jnp.asarray(index_all | (1 << bit_no), dtype=jnp.int32)
    side_bits = jnp.asarray((index_all >> bit_no) & 1, dtype=jnp.int32)
    if which_axis == 0:
        side_mask = side_bits[:, None, None, None, None]
    else:
        side_mask = side_bits[None, :, None, None, None]
    half = current.shape[4] // 2
    children = []
    for index_set in (lower_index, upper_index):
        child = jnp.take(current, index_set, axis=which_axis)
        children.append(jnp.where(side_mask == 0, child[..., :half], child[..., half:]))
    stacked = jnp.stack(children, axis=3)
    real_in = stacked[:, :, 0]
    imag_in = stacked[:, :, 1]
    real_k = interp_dir[0]
    imag_k = interp_dir[1]
    high = lax.Precision.HIGHEST
    real_out = jnp.einsum("tpcj,xycjh->xypth", real_k, real_in, precision=high) - jnp.einsum("tpcj,xycjh->xypth", imag_k, imag_in, precision=high)
    imag_out = jnp.einsum("tpcj,xycjh->xypth", real_k, imag_in, precision=high) + jnp.einsum("tpcj,xycjh->xypth", imag_k, real_in, precision=high)
    shape_out = (current.shape[0], current.shape[1], current.shape[3], current.shape[4])
    real_out = real_out.reshape(shape_out)
    imag_out = imag_out.reshape(shape_out)
    phase = node_values[None, None, :, None] * angles[:, :, None, :]
    cosine = jnp.cos(phase)
    sine_part = jnp.sin(phase)
    return jnp.stack([real_out * cosine - imag_out * sine_part, real_out * sine_part + imag_out * cosine], axis=2)


def reference(weights, phase_slope, interp_matrix, evaluation):
    current = weights
    x_bits = GX.bit_length() - 1
    y_bits = GY.bit_length() - 1
    for level_no in range(LEVELS):
        current = merge_global(current, 0, level_no % x_bits, interp_matrix[0], phase_slope[2 * level_no], cheb_nodes(0))
        current = merge_global(current, 1, level_no % y_bits, interp_matrix[1], phase_slope[2 * level_no + 1], cheb_nodes(1))
    high = lax.Precision.HIGHEST
    values = jnp.einsum("pj,xyjs->xyps", evaluation[0], current[:, :, 0], precision=high) - jnp.einsum("pj,xyjs->xyps", evaluation[1], current[:, :, 1], precision=high)
    piece = SLOTS // (GX * GY)
    values = values.reshape(GX, GY, R2, GX, GY, piece)
    values = jnp.transpose(values, (3, 4, 2, 0, 1, 5))
    return values.reshape(GX, GY, R2, SLOTS)
```

```python
import functools

import jax
import jax.numpy as jnp
import numpy as np
from jax import lax
from jax.experimental import pallas as pl
from jax.experimental.pallas import tpu as pltpu
from jax.sharding import PartitionSpec as P

AXES = ("bx", "by")
ROWS = 64
WIDE = 72
NODES = [float(np.cos(np.pi * (2 * m + 1) / 16)) for m in range(4)]
STEP_BITS = [(None, 0), (0, 1), (3, 0), (1, 1), (4, 0), (2, 1), (5, 0), (0, 1)]
F32 = jnp.float32
BF16 = jnp.bfloat16


def split_two(value):
    high = value.astype(BF16)
    low = (value - high.astype(F32)).astype(BF16)
    return high, low


def pack_kernel(w0_ref, w1_ref, p0_ref, p1_ref, out_ref):
    for pair in range(w0_ref.shape[1] // 128):
        lanes = slice(pair * 128, pair * 128 + 128)
        for top, (w_ref, p_ref) in enumerate(((w0_ref, p0_ref), (w1_ref, p1_ref))):
            turned = w_ref[:, lanes].T
            for b in range(2):
                for w in range(2):
                    out_ref[w, 2 * pair + b, 32 * top : 32 * top + 32, :] = turned[
                        64 * b + 32 * w : 64 * b + 32 * w + 32
                    ]
        s0 = p0_ref[:, lanes]
        s1 = p1_ref[:, lanes]
        for b in range(2):
            both = jnp.concatenate([s0[:, 64 * b : 64 * b + 64], s1[:, 64 * b : 64 * b + 64]], axis=1)
            for w in range(2):
                out_ref[w, 2 * pair + b, ROWS:WIDE, :] = both


def pack(weights, slopes):
    block = 512
    half = weights.shape[1] // 2 // block
    return pl.pallas_call(
        pack_kernel,
        out_shape=jax.ShapeDtypeStruct((2, 64, WIDE, 128), F32),
        grid=(half,),
        in_specs=[
            pl.BlockSpec((128, block), lambda i: (0, i)),
            pl.BlockSpec((128, block), lambda i: (0, i + half)),
            pl.BlockSpec((8, block), lambda i: (0, i)),
            pl.BlockSpec((8, block), lambda i: (0, i + half)),
        ],
        out_specs=pl.BlockSpec((2, block // 64, WIDE, 128), lambda i: (0, i, 0, 0)),
        compiler_params=pltpu.CompilerParams(vmem_limit_bytes=32 << 20),
        cost_estimate=pl.CostEstimate(flops=0, bytes_accessed=9 << 20, transcendentals=0),
    )(weights, weights, slopes, slopes)


def sincos(angle):
    h = angle * 0.5
    q = h * h
    s = q * (-1 / 39916800) + 1 / 362880
    s = s * q - 1 / 5040
    s = s * q + 1 / 120
    s = s * q - 1 / 6
    s = (s * q + 1.0) * h
    c = q * (1 / 479001600) - 1 / 3628800
    c = c * q + 1 / 40320
    c = c * q - 1 / 720
    c = c * q + 1 / 24
    c = c * q - 0.5
    c = c * q + 1.0
    return 2.0 * s * c, 1.0 - 2.0 * s * s


def lane_gather(value, index):
    return jnp.take_along_axis(value, index, axis=1, mode="promise_in_bounds")


def build_tables(w, a_ref, cos_ref, sin_ref):
    lane = lax.broadcasted_iota(jnp.int32, (32, 128), 1)
    m = lane % 4
    node = jnp.where(m == 0, NODES[0], jnp.where(m == 1, NODES[1], jnp.where(m == 2, NODES[2], NODES[3])))
    second = lane // 4 % 2 == 1
    g = lane // 8

    @pl.loop(0, 8)
    def _(step):
        slab = a_ref[pl.ds(ROWS + step, 128, stride=WIDE), :]
        turned = slab.T
        t0 = jnp.where(w == 0, turned[0:32], turned[32:64])
        t1 = jnp.where(w == 0, turned[64:96], turned[96:128])
        for tile in range(4):
            for h in range(2):
                index = ((2 * (2 * tile + g // 8) + h) * 8) + g % 8
                slope = jnp.where(second, lane_gather(t1, index), lane_gather(t0, index))
                s, c = sincos(slope * node)
                cos_ref[step * 4 + tile, 32 * h : 32 * h + 32, :] = c
                sin_ref[step * 4 + tile, 32 * h : 32 * h + 32, :] = s


def factors(step, box, direction, cos_ref, sin_ref):
    lane = lax.broadcasted_iota(jnp.int32, (ROWS, 128), 1)
    p = lane % 64
    m = p // 8 if direction == 0 else p % 8
    index = lane // 64 * 4 + jnp.where(m < 4, m, 7 - m) + (box % 16) * 8
    tile = step * 4 + box // 16
    c = lane_gather(cos_ref[tile], index)
    s = lane_gather(sin_ref[tile], index)
    return c, jnp.where(m < 4, s, -s)


def rotate(merged, c, s):
    re = merged[:, :128]
    im = merged[:, 128:]
    return re * c - im * s, re * s + im * c


def by_top(re, im):
    lower = lax.broadcasted_iota(jnp.int32, re.shape, 1) < 64
    first = jnp.where(lower, re, pltpu.roll(im, 64, 1))
    second = jnp.where(lower, pltpu.roll(re, 64, 1), im)
    return first, second


def insert_bit(q, bit, value):
    return ((q >> bit) << (bit + 1)) | (value << bit) | (q & ((1 << bit) - 1))


GROUPS = 4


def main_kernel(w_ref, a_ref, k_ref, e_ref, own_ref, send_ref, hi_ref, lo_ref, k3_ref, e3_ref, cos_ref, sin_ref):
    build_tables(w_ref[0], a_ref, cos_ref, sin_ref)
    for d in range(2):
        high, low = split_two(k_ref[d])
        k3_ref[d, 0:256] = high
        k3_ref[d, 256:512] = high
        k3_ref[d, 512:768] = low
    high, low = split_two(e_ref[...])
    e3_ref[:, 0:256] = high
    e3_ref[:, 256:512] = high
    e3_ref[:, 512:768] = low

    def store(box, re, im):
        for top, tile in enumerate(by_top(re, im)):
            high, low = split_two(tile)
            hi_ref[2 * box + top] = high
            lo_ref[2 * box + top] = low

    @pl.loop(0, 64 // (2 * GROUPS))
    def _(i):
        rows = []
        for n in range(2 * GROUPS):
            box = i * 2 * GROUPS + n
            at = box // 8 * 16 + box % 8
            parts = [split_two(a_ref[pl.ds(pl.multiple_of((at + 8 * c) * WIDE, 8), ROWS), :]) for c in range(2)]
            highs = [p[0] for p in parts]
            lows = [p[1] for p in parts]
            rows.append(jnp.concatenate(highs + lows + highs, axis=1))
        merged = jnp.dot(jnp.concatenate(rows, axis=0), k3_ref[0], preferred_element_type=F32)
        for n in range(2 * GROUPS):
            box = i * 2 * GROUPS + n
            c, s = factors(0, box, 0, cos_ref, sin_ref)
            store(box, *rotate(merged[ROWS * n : ROWS * n + ROWS], c, s))

    def gather_rows(boxes):
        rows = []
        for pair in boxes:
            for h in range(2):
                highs = [hi_ref[2 * box + h] for box in pair]
                lows = [lo_ref[2 * box + h] for box in pair]
                rows.append(jnp.concatenate(highs + lows + highs, axis=1))
        return jnp.concatenate(rows, axis=0)

    for step in range(1, 7):
        bit, direction = STEP_BITS[step]

        @pl.loop(0, 32 // GROUPS)
        def _(i, step=step, bit=bit, direction=direction):
            boxes = [[insert_bit(i * GROUPS + n, bit, c) for c in range(2)] for n in range(GROUPS)]
            merged = jnp.dot(gather_rows(boxes), k3_ref[direction], preferred_element_type=F32)
            for n in range(GROUPS):
                for h in range(2):
                    box = boxes[n][h]
                    at = ROWS * (2 * n + h)
                    c, s = factors(step, box, direction, cos_ref, sin_ref)
                    store(box, *rotate(merged[at : at + ROWS], c, s))

    @pl.loop(0, 16)
    def _(i):
        boxes = [[i * 4 + 2 * y1 + c for c in range(2)] for y1 in range(2)]
        merged = jnp.dot(gather_rows(boxes), k3_ref[1], preferred_element_type=F32)
        tiles = {}
        for y in range(4):
            c, s = factors(7, i * 4 + y, 1, cos_ref, sin_ref)
            re, im = rotate(merged[ROWS * y : ROWS * y + ROWS], c, s)
            tiles[y] = split_two(jnp.concatenate([re, im], axis=1))
        rows = []
        for h in range(2):
            for y in (0, 2, 1, 3):
                high, low = (t[32 * h : 32 * h + 32] for t in tiles[y])
                rows.append(jnp.concatenate([high, low, high], axis=1))
        field = lax.dot_general(
            e3_ref[...], jnp.concatenate(rows, axis=0), (((1,), (1,)), ((), ())), preferred_element_type=F32
        )
        for h in range(2):
            at = pl.multiple_of(((i // 2) * 4 + 2 * h + i % 2) * 128, 128)
            own_ref[:, pl.ds(at, 128)] = field[0:64, 128 * h : 128 * h + 128]
            send_ref[:, pl.ds(at, 128)] = field[64:128, 128 * h : 128 * h + 128]


def butterfly(w, arrived, k, e):
    vmem = pl.BlockSpec(memory_space=pltpu.VMEM)
    return pl.pallas_call(
        main_kernel,
        out_shape=[jax.ShapeDtypeStruct((64, 4096), F32)] * 2,
        in_specs=[pl.BlockSpec(memory_space=pltpu.SMEM), vmem, vmem, vmem],
        out_specs=[vmem, vmem],
        scratch_shapes=[
            pltpu.VMEM((128, ROWS, 128), BF16),
            pltpu.VMEM((128, ROWS, 128), BF16),
            pltpu.VMEM((2, 768, 256), BF16),
            pltpu.VMEM((128, 768), BF16),
            pltpu.VMEM((32, ROWS, 128), F32),
            pltpu.VMEM((32, ROWS, 128), F32),
        ],
        compiler_params=pltpu.CompilerParams(vmem_limit_bytes=48 << 20),
        cost_estimate=pl.CostEstimate(flops=15_000_000_000, bytes_accessed=7 << 20, transcendentals=0),
    )(w, arrived, k, e)


def join_kernel(w_ref, own_ref, got_ref, out_ref):
    first = w_ref[0] == 0
    lane = lax.broadcasted_iota(jnp.int32, (64, 128), 1)
    even = lane // 32 % 2 == 0
    for tile in range(own_ref.shape[1] // 128):
        lanes = slice(128 * tile, 128 * tile + 128)
        own = own_ref[:, lanes]
        got = got_ref[:, lanes]
        a = jnp.where(first, own, got)
        b = jnp.where(first, got, own)
        out_ref[:, 256 * tile : 256 * tile + 128] = jnp.where(even, a, pltpu.roll(b, 32, 1))
        out_ref[:, 256 * tile + 128 : 256 * tile + 256] = jnp.where(even, pltpu.roll(a, 96, 1), b)


def join(w, own, got):
    block = 1024
    return pl.pallas_call(
        join_kernel,
        out_shape=jax.ShapeDtypeStruct((64, 8192), F32),
        grid=(4096 // block,),
        in_specs=[
            pl.BlockSpec(memory_space=pltpu.SMEM),
            pl.BlockSpec((64, block), lambda i: (0, i)),
            pl.BlockSpec((64, block), lambda i: (0, i)),
        ],
        out_specs=pl.BlockSpec((64, 2 * block), lambda i: (0, i)),
        compiler_params=pltpu.CompilerParams(vmem_limit_bytes=32 << 20),
        cost_estimate=pl.CostEstimate(flops=0, bytes_accessed=4 << 20, transcendentals=0),
    )(w, own, got)


def merge_matrices(interp_matrix):
    re = jnp.transpose(interp_matrix[:, 0], (0, 3, 4, 1, 2)).reshape(2, 2, 64, 128)
    im = jnp.transpose(interp_matrix[:, 1], (0, 3, 4, 1, 2)).reshape(2, 2, 64, 128)
    from_re = jnp.concatenate([re, im], axis=3)
    from_im = jnp.concatenate([-im, re], axis=3)
    return jnp.stack([from_re, from_im], axis=2).reshape(2, 256, 256)


def evaluation_matrix(evaluation, w):
    zero = jnp.zeros((64, 64), F32)
    re, im = evaluation[0], -evaluation[1]
    low = jnp.concatenate([re, zero, im, zero], axis=1)
    high = jnp.concatenate([zero, re, zero, im], axis=1)
    return jnp.where(w == 0, jnp.concatenate([low, high], axis=0), jnp.concatenate([high, low], axis=0))


def shards(weights, phase_slope, interp_matrix, evaluation):
    w = lax.axis_index("bx") >> 3
    w_one = w.astype(jnp.int32).reshape(1)
    packed = pack(weights.reshape(128, 8192), phase_slope.reshape(8, 8192))
    arrived = lax.all_to_all(packed.reshape(128, WIDE, 128), AXES, split_axis=0, concat_axis=0, tiled=True)
    own, send = butterfly(
        w_one, arrived.reshape(128 * WIDE, 128), merge_matrices(interp_matrix), evaluation_matrix(evaluation, w)
    )
    got = lax.ppermute(send, "bx", [(i, i ^ 8) for i in range(16)])
    return join(w_one, own, got)[None, None]


def solution(mesh):
    in_specs = (P("bx", "by", None, None, None), P(None, "bx", "by", None), P(), P())
    out_specs = P("bx", "by", None, None)
    return jax.shard_map(shards, mesh=mesh, in_specs=in_specs, out_specs=out_specs, check_vma=False)
```

```python
import functools

import jax
import jax.numpy as jnp
import numpy as np
from jax import lax
from jax.experimental import pallas as pl
from jax.experimental.pallas import tpu as pltpu
from jax.sharding import PartitionSpec as P

PACK_VMEM = 60 << 20
MAIN_VMEM = 24 << 20
AXES = ("bx", "by")
ROWS = 32
SLOPES = 8
NODES = [float(np.cos(np.pi * (2 * m + 1) / 16)) for m in range(4)]
F32 = jnp.float32
BF16 = jnp.bfloat16


def split_two(value):
    high = value.astype(BF16)
    low = (value - high.astype(F32)).astype(BF16)
    return high, low


def pack_weights_kernel(w_ref, out_ref):
    for pair in range(w_ref.shape[1] // 128):
        turned = w_ref[:, pair * 128 : pair * 128 + 128].T
        for b in range(2):
            for w in range(2):
                at = 64 * b + 32 * w
                out_ref[w, 2 * pair + b, 0:ROWS, :] = turned[at : at + 32]


def pack_both_kernel(w_ref, p0_ref, p1_ref, out_ref):
    pack_weights_kernel(w_ref, out_ref)
    for b in range(w_ref.shape[1] // 64):
        both = jnp.concatenate([p_ref[:, 0, 64 * b : 64 * b + 64] for p_ref in (p0_ref, p1_ref)], axis=1)
        for w in range(2):
            out_ref[w, b, ROWS : ROWS + SLOPES, :] = both


def pack(weights, slopes, top):
    block = 512
    half = weights.shape[1] // 2 // block
    first = top * half
    if slopes is None:
        kernel, rows, more, specs = pack_weights_kernel, ROWS, [], []
    else:
        kernel, rows, more = pack_both_kernel, ROWS + SLOPES, [slopes, slopes]
        specs = [
            pl.BlockSpec((8, 1, block), lambda i: (0, 0, i)),
            pl.BlockSpec((8, 1, block), lambda i: (0, 0, i + half)),
        ]
    out = pl.pallas_call(
        kernel,
        out_shape=jax.ShapeDtypeStruct((2, 64, rows, 128), F32),
        grid=(half,),
        in_specs=[pl.BlockSpec((128, block), lambda i: (0, first + i))] + specs,
        out_specs=pl.BlockSpec((2, block // 64, rows, 128), lambda i: (0, i, 0, 0)),
        compiler_params=pltpu.CompilerParams(vmem_limit_bytes=PACK_VMEM),
        cost_estimate=pl.CostEstimate(flops=0, bytes_accessed=5 << 20, transcendentals=0),
    )(weights, *more)
    return out.reshape(128, rows, 128)


def sincos(angle):
    h = angle * 0.5
    q = h * h
    s = q * (-1 / 39916800) + 1 / 362880
    s = s * q - 1 / 5040
    s = s * q + 1 / 120
    s = s * q - 1 / 6
    s = (s * q + 1.0) * h
    c = q * (1 / 479001600) - 1 / 3628800
    c = c * q + 1 / 40320
    c = c * q - 1 / 720
    c = c * q + 1 / 24
    c = c * q - 0.5
    c = c * q + 1.0
    return 2.0 * s * c, 1.0 - 2.0 * s * s


def lane_gather(value, index):
    return jnp.take_along_axis(value, index, axis=1, mode="promise_in_bounds")


def build_tables(w, a_ref, tables):
    lane = lax.broadcasted_iota(jnp.int32, (ROWS, 128), 1)
    m = lane % 4
    node = jnp.where(m == 0, NODES[0], jnp.where(m == 1, NODES[1], jnp.where(m == 2, NODES[2], NODES[3])))
    second = lane // 4 % 2 == 1
    g = lane // 8

    @pl.loop(0, 8)
    def _(step):
        slab = a_ref[pl.ds(ROWS + step, 128, stride=ROWS + SLOPES), :]
        turned = slab.T
        t0 = jnp.where(w == 0, turned[0:32], turned[32:64])
        t1 = jnp.where(w == 0, turned[64:96], turned[96:128])
        for tile in range(4):
            for h, (cos_ref, sin_ref) in enumerate(tables):
                index = ((2 * (2 * tile + g // 8) + h) * 8) + g % 8
                slope = jnp.where(second, lane_gather(t1, index), lane_gather(t0, index))
                s, c = sincos(slope * node)
                cos_ref[step * 4 + tile] = c
                sin_ref[step * 4 + tile] = s


def factors(step, box, direction, cos_ref, sin_ref):
    lane = lax.broadcasted_iota(jnp.int32, (ROWS, 128), 1)
    p = lane % 64
    m = p // 8 if direction == 0 else p % 8
    index = lane // 64 * 4 + jnp.where(m < 4, m, 7 - m) + (box % 16) * 8
    tile = step * 4 + box // 16
    c = lane_gather(cos_ref[tile], index)
    s = lane_gather(sin_ref[tile], index)
    return c, jnp.where(m < 4, s, -s)


def rotate(merged, c, s):
    re = merged[:, :128]
    im = merged[:, 128:]
    return re * c - im * s, re * s + im * c


def by_top(re, im):
    lower = lax.broadcasted_iota(jnp.int32, re.shape, 1) < 64
    first = jnp.where(lower, re, pltpu.roll(im, 64, 1))
    second = jnp.where(lower, pltpu.roll(re, 64, 1), im)
    return first, second


def insert_bit(q, bit, value):
    return ((q >> bit) << (bit + 1)) | (value << bit) | (q & ((1 << bit) - 1))


SUB = 4


def fill_matrices(k_ref, k3_ref):
    for d in range(2):
        high, low = split_two(k_ref[d])
        k3_ref[d, 0:256] = high
        k3_ref[d, 256:512] = high
        k3_ref[d, 512:768] = low


def widen(first, second):
    return jnp.concatenate([first[0], second[0], first[1], second[1], first[0], second[0]], axis=1)


def load(state, at):
    return state[0][at], state[1][at]


def product(rows, matrix):
    return jnp.dot(jnp.concatenate(rows, axis=0), matrix, preferred_element_type=F32)


def early_steps(a_ref, stride, k_ref, cos_ref, sin_ref, outs, hi_ref, lo_ref, k3_ref):
    fill_matrices(k_ref, k3_ref)

    @pl.loop(0, 2)
    def _(i):
        for sub in range(0, 32, 2 * SUB):
            boxes = [i * 32 + sub + n for n in range(2 * SUB)]
            rows = []
            for box in boxes:
                at = box // 8 * 16 + box % 8
                rows.append(
                    widen(
                        *(
                            split_two(a_ref[pl.ds(pl.multiple_of((at + 8 * c) * stride, 8), ROWS), :])
                            for c in range(2)
                        )
                    )
                )
            merged = product(rows, k3_ref[0])
            for n, box in enumerate(boxes):
                c, s = factors(0, box, 0, cos_ref, sin_ref)
                re, im = rotate(merged[ROWS * n : ROWS * n + ROWS], c, s)
                for top, tile in enumerate(by_top(re, im)):
                    hi_ref[2 * box + top], lo_ref[2 * box + top] = split_two(tile)

    @pl.loop(0, 2)
    def _(i):
        for sub in range(0, 16, SUB):
            pairs = [i * 16 + sub + n for n in range(SUB)]
            rows = [widen(*(load((hi_ref, lo_ref), 4 * q + 2 * c + h) for c in range(2))) for q in pairs for h in range(2)]
            merged = product(rows, k3_ref[1])
            for n in range(2 * SUB):
                box = 2 * pairs[0] + n
                c, s = factors(1, box, 1, cos_ref, sin_ref)
                re, im = rotate(merged[ROWS * n : ROWS * n + ROWS], c, s)
                for top, tile in enumerate(by_top(re, im)):
                    outs[2 * top][box], outs[2 * top + 1][box] = split_two(tile)


def first_kernel(w_ref, a_ref, k_ref, *refs):
    outs, (cos0_ref, sin0_ref, cos1_ref, sin1_ref), scratch = refs[:4], refs[4:8], refs[8:]
    build_tables(w_ref[0], a_ref, ((cos0_ref, sin0_ref), (cos1_ref, sin1_ref)))
    early_steps(a_ref, ROWS + SLOPES, k_ref, cos0_ref, sin0_ref, outs, *scratch)


def second_kernel(a_ref, k_ref, cos_ref, sin_ref, *refs):
    early_steps(a_ref, ROWS, k_ref, cos_ref, sin_ref, refs[:4], *refs[4:])


def late_kernel(
    x1, hi_ref, lo_ref, k_ref, e_ref, cos_ref, sin_ref, own_ref, send_ref, hi0_ref, lo0_ref, hi1_ref, lo1_ref, k3_ref, e3_ref
):
    fill_matrices(k_ref, k3_ref)
    high, low = split_two(e_ref[...])
    e3_ref[:, 0:256] = high
    e3_ref[:, 256:512] = high
    e3_ref[:, 512:768] = low
    states = ((hi0_ref, lo0_ref), (hi1_ref, lo1_ref))

    def finish(merged, n, step, box, direction):
        c, s = factors(step, insert_bit(box, 3, x1), direction, cos_ref, sin_ref)
        return rotate(merged[ROWS * n : ROWS * n + ROWS], c, s)

    def store(state, box, re, im):
        for top, tile in enumerate(by_top(re, im)):
            state[0][2 * box + top], state[1][2 * box + top] = split_two(tile)

    for sub in range(0, 32, 2 * SUB):
        boxes = range(sub, sub + 2 * SUB)
        rows = [widen(*(load((hi_ref, lo_ref), insert_bit(box, 3, c)) for c in range(2))) for box in boxes]
        merged = product(rows, k3_ref[0])
        for n, box in enumerate(boxes):
            store(states[0], box, *finish(merged, n, 2, box, 0))

    def middle(step, bit, direction, source, target):
        for sub in range(0, 16, SUB):
            pairs = [[insert_bit(sub + n, bit, c) for c in range(2)] for n in range(SUB)]
            rows = [widen(*(load(source, 2 * box + h) for box in pair)) for pair in pairs for h in range(2)]
            merged = product(rows, k3_ref[direction])
            for n in range(2 * SUB):
                box = pairs[n // 2][n % 2]
                store(target, box, *finish(merged, n, step, box, direction))

    @pl.loop(0, 2)
    def _(level):
        middle(2 * level + 3, level + 1, 1, states[0], states[1])
        middle(2 * level + 4, level + 3, 0, states[1], states[0])

    for sub in range(0, 16, SUB):
        boxes = [[2 * (sub + n) + c for c in range(2)] for n in range(SUB)]
        rows = [widen(*(load(states[0], 2 * box + h) for box in pair)) for pair in boxes for h in range(2)]
        merged = product(rows, k3_ref[1])
        rows = [None] * (2 * SUB)
        for n in range(2 * SUB):
            high, low = split_two(jnp.concatenate(finish(merged, n, 7, 2 * sub + n, 1), axis=1))
            rows[n // 4 * 4 + (0, 2, 1, 3)[n % 4]] = jnp.concatenate([high, low, high], axis=1)
        field = lax.dot_general(
            e3_ref[...], jnp.concatenate(rows, axis=0), (((1,), (1,)), ((), ())), preferred_element_type=F32
        )
        own_ref[:, 64 * sub : 64 * sub + 64 * SUB] = field[0:64]
        send_ref[:, 64 * sub : 64 * sub + 64 * SUB] = field[64:128]


VMEM = pl.BlockSpec(memory_space=pltpu.VMEM)
TABLE = jax.ShapeDtypeStruct((32, ROWS, 128), F32)
HALF = jax.ShapeDtypeStruct((64, ROWS, 128), BF16)
FIELD = jax.ShapeDtypeStruct((64, 1024), F32)
MATRICES = pltpu.VMEM((2, 768, 256), BF16)


def cost(flops):
    return pl.CostEstimate(flops=flops, bytes_accessed=4 << 20, transcendentals=0)


def first_part(w, arrived, k):
    return pl.pallas_call(
        first_kernel,
        out_shape=[HALF] * 4 + [TABLE] * 4,
        in_specs=[pl.BlockSpec(memory_space=pltpu.SMEM), VMEM, VMEM],
        out_specs=[VMEM] * 8,
        scratch_shapes=[pltpu.VMEM((128, ROWS, 128), BF16)] * 2 + [MATRICES],
        compiler_params=pltpu.CompilerParams(vmem_limit_bytes=MAIN_VMEM),
        cost_estimate=cost(4_000_000_000),
    )(w, arrived, k)


def second_part(arrived, k, cos, sin):
    return pl.pallas_call(
        second_kernel,
        out_shape=[HALF] * 4,
        in_specs=[VMEM] * 4,
        out_specs=[VMEM] * 4,
        scratch_shapes=[pltpu.VMEM((128, ROWS, 128), BF16)] * 2 + [MATRICES],
        compiler_params=pltpu.CompilerParams(vmem_limit_bytes=MAIN_VMEM),
        cost_estimate=cost(3_000_000_000),
    )(arrived, k, cos, sin)


def late_part(x1, high, low, k, e, cos, sin):
    return pl.pallas_call(
        functools.partial(late_kernel, x1),
        out_shape=[FIELD, FIELD],
        in_specs=[VMEM] * 6,
        out_specs=[VMEM] * 2,
        scratch_shapes=[pltpu.VMEM((64, ROWS, 128), BF16)] * 4 + [MATRICES, pltpu.VMEM((128, 768), BF16)],
        compiler_params=pltpu.CompilerParams(vmem_limit_bytes=MAIN_VMEM),
        cost_estimate=cost(5_000_000_000),
    )(high, low, k, e, cos, sin)


def join_kernel(place, w_ref, own_ref, got_ref, *rest):
    out_ref, held_ref, sems = rest[-3:]
    first = w_ref[0] == 0
    lane = lax.broadcasted_iota(jnp.int32, (64, 128), 1)
    even = lane // 32 % 2 == 0
    copies = []
    for box in range(4):
        for y2 in range(2):
            lanes = slice(256 * box + 128 * y2, 256 * box + 128 * y2 + 128)
            own = own_ref[:, lanes]
            got = got_ref[:, lanes]
            a = jnp.where(first, own, got)
            b = jnp.where(first, got, own)
            held_ref[box, :, 256 * y2 : 256 * y2 + 128] = jnp.where(even, a, pltpu.roll(b, 32, 1))
            held_ref[box, :, 256 * y2 + 128 : 256 * y2 + 256] = jnp.where(even, pltpu.roll(a, 96, 1), b)
        at = (4 * box + place) * 512
        copies.append(pltpu.make_async_copy(held_ref.at[box], out_ref.at[:, at : at + 512], sems.at[box]))
        copies[-1].start()
    for copy in copies:
        copy.wait()


def join(w, own, got, place, out):
    more = [] if out is None else [out]
    anywhere = pl.BlockSpec(memory_space=pl.ANY)
    return pl.pallas_call(
        functools.partial(join_kernel, place),
        out_shape=jax.ShapeDtypeStruct((64, 8192), F32),
        in_specs=[pl.BlockSpec(memory_space=pltpu.SMEM), VMEM, VMEM] + [anywhere] * len(more),
        out_specs=anywhere,
        scratch_shapes=[pltpu.VMEM((4, 64, 512), F32), pltpu.SemaphoreType.DMA((4,))],
        input_output_aliases={3: 0} if more else {},
        compiler_params=pltpu.CompilerParams(vmem_limit_bytes=MAIN_VMEM),
        cost_estimate=pl.CostEstimate(flops=0, bytes_accessed=1 << 20, transcendentals=0),
    )(w, own, got, *more)


def merge_matrices(interp_matrix):
    re = jnp.transpose(interp_matrix[:, 0], (0, 3, 4, 1, 2)).reshape(2, 2, 64, 128)
    im = jnp.transpose(interp_matrix[:, 1], (0, 3, 4, 1, 2)).reshape(2, 2, 64, 128)
    from_re = jnp.concatenate([re, im], axis=3)
    from_im = jnp.concatenate([-im, re], axis=3)
    return jnp.stack([from_re, from_im], axis=2).reshape(2, 256, 256)


def evaluation_matrix(evaluation, w):
    zero = jnp.zeros((64, 64), F32)
    re, im = evaluation[0], -evaluation[1]
    low = jnp.concatenate([re, zero, im, zero], axis=1)
    high = jnp.concatenate([zero, re, zero, im], axis=1)
    return jnp.where(w == 0, jnp.concatenate([low, high], axis=0), jnp.concatenate([high, low], axis=0))


def shards(weights, phase_slope, interp_matrix, evaluation):
    w = lax.axis_index("bx") >> 3
    w_one = w.astype(jnp.int32).reshape(1)
    planes = weights.reshape(128, 8192)
    k = merge_matrices(interp_matrix)
    e = evaluation_matrix(evaluation, w)

    def spread(packed):
        return lax.all_to_all(packed, AXES, split_axis=0, concat_axis=0, tiled=True).reshape(-1, 128)

    def swap(field):
        return lax.ppermute(field, "bx", [(i, i ^ 8) for i in range(16)])

    arrived0 = spread(pack(planes, phase_slope.reshape(8, 1, 8192), 0))
    arrived1 = spread(pack(planes, None, 1))
    out = None
    for top in range(2):
        if top == 0:
            *halves, cos, sin, cos1, sin1 = first_part(w_one, arrived0, k)
        else:
            cos, sin = cos1, sin1
            halves = second_part(arrived1, k, cos, sin)
        for x1 in range(2):
            own, send = late_part(x1, halves[2 * x1], halves[2 * x1 + 1], k, e, cos, sin)
            out = join(w_one, own, swap(send), 2 * x1 + top, out)
    return out[None, None]


def solution(mesh):
    in_specs = (P("bx", "by", None, None, None), P(None, "bx", "by", None), P(), P())
    out_specs = P("bx", "by", None, None)
    return jax.shard_map(shards, mesh=mesh, in_specs=in_specs, out_specs=out_specs, check_vma=False)
```

```python
import functools

import jax
import jax.numpy as jnp
import numpy as np
from jax import lax
from jax.experimental import pallas as pl
from jax.experimental.pallas import tpu as pltpu
from jax.sharding import PartitionSpec as P

PACK_VMEM = 60 << 20
PACK_BLOCK = 1024
MAIN_VMEM = 24 << 20
AXES = ("bx", "by")
ROWS = 32
SLOPES = 4
NODES = [float(np.cos(np.pi * (2 * m + 1) / 16)) for m in range(4)]
F32 = jnp.float32
BF16 = jnp.bfloat16


def split_two(value):
    high = value.astype(BF16)
    low = (value - high.astype(F32)).astype(BF16)
    return high, low


def pack_kernel(w_ref, *refs):
    *slopes, out_ref = refs
    rows = ROWS + SLOPES * (len(slopes) > 0)
    for pair in range(w_ref.shape[1] // 128):
        turned = w_ref[:, pair * 128 : pair * 128 + 128].T
        for b in range(2):
            for w in range(2):
                at = 64 * b + 32 * w
                to = (2 * pair + b) * rows
                out_ref[w, to : to + ROWS, :] = turned[at : at + 32]
    if slopes:
        p0 = slopes[0][:, 0, :]
        p1 = slopes[1][:, 0, :]
        for b in range(w_ref.shape[1] // 64):
            for w in range(2):
                at = slice(64 * b + 32 * w, 64 * b + 32 * w + 32)
                parts = [p0[0:4, at], p1[0:4, at], p0[4:8, at], p1[4:8, at]]
                out_ref[w, b * rows + ROWS : b * rows + rows, :] = jnp.concatenate(parts, axis=1)


def pack(weights, slopes, top):
    block = PACK_BLOCK
    half = weights.shape[1] // 2 // block
    first = top * half
    rows, more, specs = ROWS, [], []
    if slopes is not None:
        rows, more = ROWS + SLOPES, [slopes, slopes]
        specs = [
            pl.BlockSpec((8, 1, block), lambda i: (0, 0, i)),
            pl.BlockSpec((8, 1, block), lambda i: (0, 0, i + half)),
        ]
    return pl.pallas_call(
        pack_kernel,
        out_shape=jax.ShapeDtypeStruct((2, 64 * rows, 128), F32),
        grid=(half,),
        in_specs=[pl.BlockSpec((128, block), lambda i: (0, first + i))] + specs,
        out_specs=pl.BlockSpec((2, block // 64 * rows, 128), lambda i: (0, i, 0)),
        compiler_params=pltpu.CompilerParams(vmem_limit_bytes=PACK_VMEM),
        cost_estimate=pl.CostEstimate(flops=0, bytes_accessed=5 << 20, transcendentals=0),
    )(weights, *more)


def sincos(angle):
    h = angle * 0.5
    q = h * h
    s = q * (-1 / 39916800) + 1 / 362880
    s = s * q - 1 / 5040
    s = s * q + 1 / 120
    s = s * q - 1 / 6
    s = (s * q + 1.0) * h
    c = q * (1 / 479001600) - 1 / 3628800
    c = c * q + 1 / 40320
    c = c * q - 1 / 720
    c = c * q + 1 / 24
    c = c * q - 0.5
    c = c * q + 1.0
    return 2.0 * s * c, 1.0 - 2.0 * s * s


def lane_gather(value, index):
    return jnp.take_along_axis(value, index, axis=1, mode="promise_in_bounds")


def build_tables(a_ref, tables):
    lane = lax.broadcasted_iota(jnp.int32, (ROWS, 128), 1)
    m = lane % 4
    node = jnp.where(m == 0, NODES[0], jnp.where(m == 1, NODES[1], jnp.where(m == 2, NODES[2], NODES[3])))
    second = lane // 4 % 2 == 1
    g = lane // 8

    @pl.loop(0, SLOPES)
    def _(row):
        turned = a_ref[pl.ds(ROWS + row, 128, stride=ROWS + SLOPES), :].T
        for late in range(2):
            t0 = turned[64 * late : 64 * late + 32]
            t1 = turned[64 * late + 32 : 64 * late + 64]
            for tile in range(4):
                for h, (cos_ref, sin_ref) in enumerate(tables):
                    index = ((2 * (2 * tile + g // 8) + h) * 8) + g % 8
                    slope = jnp.where(second, lane_gather(t1, index), lane_gather(t0, index))
                    s, c = sincos(slope * node)
                    at = (row + SLOPES * late) * 4 + tile
                    cos_ref[at] = c
                    sin_ref[at] = s


def factors(step, box, direction, cos_ref, sin_ref):
    lane = lax.broadcasted_iota(jnp.int32, (ROWS, 128), 1)
    p = lane % 64
    m = p // 8 if direction == 0 else p % 8
    index = lane // 64 * 4 + jnp.where(m < 4, m, 7 - m) + (box % 16) * 8
    tile = step * 4 + box // 16
    c = lane_gather(cos_ref[tile], index)
    s = lane_gather(sin_ref[tile], index)
    return c, jnp.where(m < 4, s, -s)


def rotate(merged, c, s):
    re = merged[:, :128]
    im = merged[:, 128:]
    return re * c - im * s, re * s + im * c


def by_top(re, im):
    lower = lax.broadcasted_iota(jnp.int32, re.shape, 1) < 64
    first = jnp.where(lower, re, pltpu.roll(im, 64, 1))
    second = jnp.where(lower, pltpu.roll(re, 64, 1), im)
    return first, second


def insert_bit(q, bit, value):
    return ((q >> bit) << (bit + 1)) | (value << bit) | (q & ((1 << bit) - 1))


SUB = 4


def fill_matrices(k_ref, k3_ref):
    for d in range(2):
        high, low = split_two(k_ref[d])
        k3_ref[d, 0:256] = high
        k3_ref[d, 256:512] = high
        k3_ref[d, 512:768] = low


def widen(first, second):
    return jnp.concatenate([first[0], second[0], first[1], second[1], first[0], second[0]], axis=1)


def load(state, at):
    return state[0][at], state[1][at]


def product(rows, matrix):
    return jnp.dot(jnp.concatenate(rows, axis=0), matrix, preferred_element_type=F32)


def early_steps(a_ref, stride, k_ref, cos_ref, sin_ref, outs, hi_ref, lo_ref, k3_ref):
    fill_matrices(k_ref, k3_ref)

    def arrived(pair, odd):
        at = pl.multiple_of(pair * 2 * stride, 8)
        if stride % 8 == 0:
            return a_ref[pl.ds(at + odd * stride, ROWS), :]
        shift = odd * stride % 8
        return a_ref[pl.ds(at + (odd * stride - shift), ROWS + 2 * shift), :][shift : shift + ROWS]

    @pl.loop(0, 2)
    def _(i):
        for sub in range(0, 32, 2 * SUB):
            boxes = [i * 32 + sub + n for n in range(2 * SUB)]
            rows = []
            for n in range(2 * SUB):
                pair = (i * 32 + sub) // 8 * 8 + n // 2 + sub % 8 // 2
                rows.append(widen(*(split_two(arrived(pair + 4 * c, n % 2)) for c in range(2))))
            merged = product(rows, k3_ref[0])
            for n, box in enumerate(boxes):
                c, s = factors(0, box, 0, cos_ref, sin_ref)
                re, im = rotate(merged[ROWS * n : ROWS * n + ROWS], c, s)
                for top, tile in enumerate(by_top(re, im)):
                    hi_ref[2 * box + top], lo_ref[2 * box + top] = split_two(tile)

    @pl.loop(0, 2)
    def _(i):
        for sub in range(0, 16, SUB):
            pairs = [i * 16 + sub + n for n in range(SUB)]
            rows = [widen(*(load((hi_ref, lo_ref), 4 * q + 2 * c + h) for c in range(2))) for q in pairs for h in range(2)]
            merged = product(rows, k3_ref[1])
            for n in range(2 * SUB):
                box = 2 * pairs[0] + n
                c, s = factors(1, box, 1, cos_ref, sin_ref)
                re, im = rotate(merged[ROWS * n : ROWS * n + ROWS], c, s)
                for top, tile in enumerate(by_top(re, im)):
                    outs[2 * top][box], outs[2 * top + 1][box] = split_two(tile)


def first_kernel(a_ref, k_ref, *refs):
    outs, (cos0_ref, sin0_ref, cos1_ref, sin1_ref), scratch = refs[:4], refs[4:8], refs[8:]
    build_tables(a_ref, ((cos0_ref, sin0_ref), (cos1_ref, sin1_ref)))
    early_steps(a_ref, ROWS + SLOPES, k_ref, cos0_ref, sin0_ref, outs, *scratch)


def second_kernel(a_ref, k_ref, cos_ref, sin_ref, *refs):
    early_steps(a_ref, ROWS, k_ref, cos_ref, sin_ref, refs[:4], *refs[4:])


def late_kernel(
    x1, hi_ref, lo_ref, k_ref, e_ref, cos_ref, sin_ref, own_ref, send_ref, hi0_ref, lo0_ref, hi1_ref, lo1_ref, k3_ref, e3_ref
):
    fill_matrices(k_ref, k3_ref)
    high, low = split_two(e_ref[...])
    e3_ref[:, 0:256] = high
    e3_ref[:, 256:512] = high
    e3_ref[:, 512:768] = low
    states = ((hi0_ref, lo0_ref), (hi1_ref, lo1_ref))

    def finish(merged, n, step, box, direction):
        c, s = factors(step, insert_bit(box, 3, x1), direction, cos_ref, sin_ref)
        return rotate(merged[ROWS * n : ROWS * n + ROWS], c, s)

    def store(state, box, re, im):
        for top, tile in enumerate(by_top(re, im)):
            state[0][2 * box + top], state[1][2 * box + top] = split_two(tile)

    for sub in range(0, 32, 2 * SUB):
        boxes = range(sub, sub + 2 * SUB)
        rows = [widen(*(load((hi_ref, lo_ref), insert_bit(box, 3, c)) for c in range(2))) for box in boxes]
        merged = product(rows, k3_ref[0])
        for n, box in enumerate(boxes):
            store(states[0], box, *finish(merged, n, 2, box, 0))

    def middle(step, bit, direction, source, target):
        for sub in range(0, 16, SUB):
            pairs = [[insert_bit(sub + n, bit, c) for c in range(2)] for n in range(SUB)]
            rows = [widen(*(load(source, 2 * box + h) for box in pair)) for pair in pairs for h in range(2)]
            merged = product(rows, k3_ref[direction])
            for n in range(2 * SUB):
                box = pairs[n // 2][n % 2]
                store(target, box, *finish(merged, n, step, box, direction))

    @pl.loop(0, 2)
    def _(level):
        middle(2 * level + 3, level + 1, 1, states[0], states[1])
        middle(2 * level + 4, level + 3, 0, states[1], states[0])

    for sub in range(0, 16, SUB):
        boxes = [[2 * (sub + n) + c for c in range(2)] for n in range(SUB)]
        rows = [widen(*(load(states[0], 2 * box + h) for box in pair)) for pair in boxes for h in range(2)]
        merged = product(rows, k3_ref[1])
        rows = [None] * (2 * SUB)
        for n in range(2 * SUB):
            high, low = split_two(jnp.concatenate(finish(merged, n, 7, 2 * sub + n, 1), axis=1))
            rows[n // 4 * 4 + (0, 2, 1, 3)[n % 4]] = jnp.concatenate([high, low, high], axis=1)
        field = lax.dot_general(
            e3_ref[...], jnp.concatenate(rows, axis=0), (((1,), (1,)), ((), ())), preferred_element_type=F32
        )
        own_ref[:, 64 * sub : 64 * sub + 64 * SUB] = field[0:64]
        send_ref[:, 64 * sub : 64 * sub + 64 * SUB] = field[64:128]


VMEM = pl.BlockSpec(memory_space=pltpu.VMEM)
TABLE = jax.ShapeDtypeStruct((32, ROWS, 128), F32)
HALF = jax.ShapeDtypeStruct((64, ROWS, 128), BF16)
FIELD = jax.ShapeDtypeStruct((64, 1024), F32)
MATRICES = pltpu.VMEM((2, 768, 256), BF16)


def cost(flops):
    return pl.CostEstimate(flops=flops, bytes_accessed=4 << 20, transcendentals=0)


def first_part(arrived, k):
    return pl.pallas_call(
        first_kernel,
        out_shape=[HALF] * 4 + [TABLE] * 4,
        in_specs=[VMEM, VMEM],
        out_specs=[VMEM] * 8,
        scratch_shapes=[pltpu.VMEM((128, ROWS, 128), BF16)] * 2 + [MATRICES],
        compiler_params=pltpu.CompilerParams(vmem_limit_bytes=MAIN_VMEM),
        cost_estimate=cost(4_000_000_000),
    )(arrived, k)


def second_part(arrived, k, cos, sin):
    return pl.pallas_call(
        second_kernel,
        out_shape=[HALF] * 4,
        in_specs=[VMEM] * 4,
        out_specs=[VMEM] * 4,
        scratch_shapes=[pltpu.VMEM((128, ROWS, 128), BF16)] * 2 + [MATRICES],
        compiler_params=pltpu.CompilerParams(vmem_limit_bytes=MAIN_VMEM),
        cost_estimate=cost(3_000_000_000),
    )(arrived, k, cos, sin)


def late_part(x1, high, low, k, e, cos, sin):
    return pl.pallas_call(
        functools.partial(late_kernel, x1),
        out_shape=[FIELD, FIELD],
        in_specs=[VMEM] * 6,
        out_specs=[VMEM] * 2,
        scratch_shapes=[pltpu.VMEM((64, ROWS, 128), BF16)] * 4 + [MATRICES, pltpu.VMEM((128, 768), BF16)],
        compiler_params=pltpu.CompilerParams(vmem_limit_bytes=MAIN_VMEM),
        cost_estimate=cost(5_000_000_000),
    )(high, low, k, e, cos, sin)


def join_kernel(place, w_ref, own_ref, got_ref, *rest):
    out_ref, held_ref, sems = rest[-3:]
    first = w_ref[0] == 0
    lane = lax.broadcasted_iota(jnp.int32, (64, 128), 1)
    even = lane // 32 % 2 == 0
    copies = []
    for box in range(4):
        for y2 in range(2):
            lanes = slice(256 * box + 128 * y2, 256 * box + 128 * y2 + 128)
            own = own_ref[:, lanes]
            got = got_ref[:, lanes]
            a = jnp.where(first, own, got)
            b = jnp.where(first, got, own)
            held_ref[box, :, 256 * y2 : 256 * y2 + 128] = jnp.where(even, a, pltpu.roll(b, 32, 1))
            held_ref[box, :, 256 * y2 + 128 : 256 * y2 + 256] = jnp.where(even, pltpu.roll(a, 96, 1), b)
        at = (4 * box + place) * 512
        copies.append(pltpu.make_async_copy(held_ref.at[box], out_ref.at[:, at : at + 512], sems.at[box]))
        copies[-1].start()
    for copy in copies:
        copy.wait()


def join(w, own, got, place, out):
    more = [] if out is None else [out]
    anywhere = pl.BlockSpec(memory_space=pl.ANY)
    return pl.pallas_call(
        functools.partial(join_kernel, place),
        out_shape=jax.ShapeDtypeStruct((64, 8192), F32),
        in_specs=[pl.BlockSpec(memory_space=pltpu.SMEM), VMEM, VMEM] + [anywhere] * len(more),
        out_specs=anywhere,
        scratch_shapes=[pltpu.VMEM((4, 64, 512), F32), pltpu.SemaphoreType.DMA((4,))],
        input_output_aliases={3: 0} if more else {},
        compiler_params=pltpu.CompilerParams(vmem_limit_bytes=MAIN_VMEM),
        cost_estimate=pl.CostEstimate(flops=0, bytes_accessed=1 << 20, transcendentals=0),
    )(w, own, got, *more)


def merge_matrices(interp_matrix):
    re = jnp.transpose(interp_matrix[:, 0], (0, 3, 4, 1, 2)).reshape(2, 2, 64, 128)
    im = jnp.transpose(interp_matrix[:, 1], (0, 3, 4, 1, 2)).reshape(2, 2, 64, 128)
    from_re = jnp.concatenate([re, im], axis=3)
    from_im = jnp.concatenate([-im, re], axis=3)
    return jnp.stack([from_re, from_im], axis=2).reshape(2, 256, 256)


def evaluation_matrix(evaluation, w):
    zero = jnp.zeros((64, 64), F32)
    re, im = evaluation[0], -evaluation[1]
    low = jnp.concatenate([re, zero, im, zero], axis=1)
    high = jnp.concatenate([zero, re, zero, im], axis=1)
    return jnp.where(w == 0, jnp.concatenate([low, high], axis=0), jnp.concatenate([high, low], axis=0))


def shards(weights, phase_slope, interp_matrix, evaluation):
    w = lax.axis_index("bx") >> 3
    w_one = w.astype(jnp.int32).reshape(1)
    planes = weights.reshape(128, 8192)
    k = merge_matrices(interp_matrix)
    e = evaluation_matrix(evaluation, w)

    def spread(packed):
        return lax.all_to_all(packed.reshape(128, 1, -1), AXES, split_axis=0, concat_axis=0, tiled=True).reshape(-1, 128)

    def swap(field):
        return lax.ppermute(field, "bx", [(i, i ^ 8) for i in range(16)])

    arrived0 = spread(pack(planes, phase_slope.reshape(8, 1, 8192), 0))
    arrived1 = spread(pack(planes, None, 1))
    out = None
    for top in range(2):
        if top == 0:
            *halves, cos, sin, cos1, sin1 = first_part(arrived0, k)
        else:
            cos, sin = cos1, sin1
            halves = second_part(arrived1, k, cos, sin)
        for x1 in range(2):
            own, send = late_part(x1, halves[2 * x1], halves[2 * x1 + 1], k, e, cos, sin)
            out = join(w_one, own, swap(send), 2 * x1 + top, out)
    return out[None, None]


def solution(mesh):
    in_specs = (P("bx", "by", None, None, None), P(None, "bx", "by", None), P(), P())
    out_specs = P("bx", "by", None, None)
    return jax.shard_map(shards, mesh=mesh, in_specs=in_specs, out_specs=out_specs, check_vma=False)
```

```python
import functools

import jax
import jax.numpy as jnp
import numpy as np
from jax import lax
from jax.experimental import pallas as pl
from jax.experimental.pallas import tpu as pltpu
from jax.sharding import PartitionSpec as P

PACK_VMEM = 60 << 20
MAIN_VMEM = 24 << 20
AXES = ("bx", "by")
ROWS = 32
SLOPES = 4
NODES = [float(np.cos(np.pi * (2 * m + 1) / 16)) for m in range(4)]
F32 = jnp.float32
BF16 = jnp.bfloat16


def split_two(value):
    high = value.astype(BF16)
    low = (value - high.astype(F32)).astype(BF16)
    return high, low


def pack_kernel(top, rows, w_ref, *refs):
    p_ref = refs[0] if rows > ROWS else None
    out_ref, held_ref, made_ref, p_held_ref, in_sems, out_sems = refs[-6:]
    pieces, _, lanes = held_ref.shape
    half = pieces * lanes
    tall = lanes // 64 * rows

    def incoming(n):
        at = pl.ds(pl.multiple_of(top * half + n * lanes, 128), lanes)
        return pltpu.make_async_copy(w_ref.at[:, at], held_ref.at[n], in_sems.at[n])

    def outgoing(n, w):
        at = pl.ds(pl.multiple_of(n * tall, 8), tall)
        return pltpu.make_async_copy(made_ref.at[w, at], out_ref.at[w, at], out_sems.at[n, w])

    more = []
    if p_ref is not None:
        more = [pltpu.make_async_copy(p_ref, p_held_ref, in_sems.at[pieces])]
        more[0].start()
    for n in range(pieces):
        incoming(n).start()
    for copy in more:
        copy.wait()

    @pl.loop(0, pieces)
    def _(n):
        incoming(n).wait()
        first = pl.multiple_of(n * tall, 8)
        for pair in range(lanes // 128):
            turned = held_ref[n, :, pair * 128 : pair * 128 + 128].T
            for b in range(2):
                for w in range(2):
                    at = 64 * b + 32 * w
                    made_ref[w, pl.ds(first + (2 * pair + b) * rows, ROWS), :] = turned[at : at + 32]
        if p_ref is not None:
            p0 = p_held_ref[:, 0, pl.ds(pl.multiple_of(n * lanes, 128), lanes)]
            p1 = p_held_ref[:, 0, pl.ds(pl.multiple_of(half + n * lanes, 128), lanes)]
            for b in range(lanes // 64):
                for w in range(2):
                    at = slice(64 * b + 32 * w, 64 * b + 32 * w + 32)
                    parts = [p0[0:4, at], p1[0:4, at], p0[4:8, at], p1[4:8, at]]
                    to = first + (b * rows + ROWS)
                    made_ref[w, pl.ds(to, SLOPES), :] = jnp.concatenate(parts, axis=1)
        for w in range(2):
            outgoing(n, w).start()

    @pl.loop(0, pieces)
    def _(n):
        for w in range(2):
            outgoing(n, w).wait()


def pack(weights, slopes, top):
    pieces, lanes = 8, 512
    rows = ROWS if slopes is None else ROWS + SLOPES
    more = [] if slopes is None else [slopes]
    anywhere = pl.BlockSpec(memory_space=pl.ANY)
    return pl.pallas_call(
        functools.partial(pack_kernel, top, rows),
        out_shape=jax.ShapeDtypeStruct((2, 64 * rows, 128), F32),
        in_specs=[anywhere] * (1 + len(more)),
        out_specs=anywhere,
        scratch_shapes=[
            pltpu.VMEM((pieces, 128, lanes), F32),
            pltpu.VMEM((2, 64 * rows, 128), F32),
            pltpu.VMEM((8, 1, 8192), F32),
            pltpu.SemaphoreType.DMA((pieces + 1,)),
            pltpu.SemaphoreType.DMA((pieces, 2)),
        ],
        compiler_params=pltpu.CompilerParams(vmem_limit_bytes=PACK_VMEM),
        cost_estimate=pl.CostEstimate(flops=0, bytes_accessed=5 << 20, transcendentals=0),
    )(weights, *more)


def sincos(angle):
    h = angle * 0.5
    q = h * h
    s = q * (-1 / 39916800) + 1 / 362880
    s = s * q - 1 / 5040
    s = s * q + 1 / 120
    s = s * q - 1 / 6
    s = (s * q + 1.0) * h
    c = q * (1 / 479001600) - 1 / 3628800
    c = c * q + 1 / 40320
    c = c * q - 1 / 720
    c = c * q + 1 / 24
    c = c * q - 0.5
    c = c * q + 1.0
    return 2.0 * s * c, 1.0 - 2.0 * s * s


def lane_gather(value, index):
    return jnp.take_along_axis(value, index, axis=1, mode="promise_in_bounds")


def build_tables(a_ref, tables):
    lane = lax.broadcasted_iota(jnp.int32, (ROWS, 128), 1)
    m = lane % 4
    node = jnp.where(m == 0, NODES[0], jnp.where(m == 1, NODES[1], jnp.where(m == 2, NODES[2], NODES[3])))
    second = lane // 4 % 2 == 1
    g = lane // 8

    @pl.loop(0, SLOPES)
    def _(row):
        turned = a_ref[pl.ds(ROWS + row, 128, stride=ROWS + SLOPES), :].T
        for late in range(2):
            t0 = turned[64 * late : 64 * late + 32]
            t1 = turned[64 * late + 32 : 64 * late + 64]
            for tile in range(4):
                for h, (cos_ref, sin_ref) in enumerate(tables):
                    index = ((2 * (2 * tile + g // 8) + h) * 8) + g % 8
                    slope = jnp.where(second, lane_gather(t1, index), lane_gather(t0, index))
                    s, c = sincos(slope * node)
                    at = (row + SLOPES * late) * 4 + tile
                    cos_ref[at] = c
                    sin_ref[at] = s


def factors(step, box, direction, cos_ref, sin_ref):
    lane = lax.broadcasted_iota(jnp.int32, (ROWS, 128), 1)
    p = lane % 64
    m = p // 8 if direction == 0 else p % 8
    index = lane // 64 * 4 + jnp.where(m < 4, m, 7 - m) + (box % 16) * 8
    tile = step * 4 + box // 16
    c = lane_gather(cos_ref[tile], index)
    s = lane_gather(sin_ref[tile], index)
    return c, jnp.where(m < 4, s, -s)


def rotate(merged, c, s):
    re = merged[:, :128]
    im = merged[:, 128:]
    return re * c - im * s, re * s + im * c


def by_top(re, im):
    lower = lax.broadcasted_iota(jnp.int32, re.shape, 1) < 64
    first = jnp.where(lower, re, pltpu.roll(im, 64, 1))
    second = jnp.where(lower, pltpu.roll(re, 64, 1), im)
    return first, second


def insert_bit(q, bit, value):
    return ((q >> bit) << (bit + 1)) | (value << bit) | (q & ((1 << bit) - 1))


SUB = 4


def fill_matrices(k_ref, k3_ref):
    for d in range(2):
        high, low = split_two(k_ref[d])
        k3_ref[d, 0:256] = high
        k3_ref[d, 256:512] = high
        k3_ref[d, 512:768] = low


def widen(first, second):
    return jnp.concatenate([first[0], second[0], first[1], second[1], first[0], second[0]], axis=1)


def load(state, at):
    return state[0][at], state[1][at]


def product(rows, matrix):
    return jnp.dot(jnp.concatenate(rows, axis=0), matrix, preferred_element_type=F32)


def early_steps(a_ref, stride, k_ref, cos_ref, sin_ref, outs, hi_ref, lo_ref, k3_ref, ready=lambda i: None):
    fill_matrices(k_ref, k3_ref)

    def arrived(pair, odd):
        at = pl.multiple_of(pair * 2 * stride, 8)
        if stride % 8 == 0:
            return a_ref[pl.ds(at + odd * stride, ROWS), :]
        shift = odd * stride % 8
        return a_ref[pl.ds(at + (odd * stride - shift), ROWS + 2 * shift), :][shift : shift + ROWS]

    @pl.loop(0, 2)
    def _(i):
        ready(i)
        for sub in range(0, 32, 2 * SUB):
            boxes = [i * 32 + sub + n for n in range(2 * SUB)]
            rows = []
            for n in range(2 * SUB):
                pair = (i * 32 + sub) // 8 * 8 + n // 2 + sub % 8 // 2
                rows.append(widen(*(split_two(arrived(pair + 4 * c, n % 2)) for c in range(2))))
            merged = product(rows, k3_ref[0])
            for n, box in enumerate(boxes):
                c, s = factors(0, box, 0, cos_ref, sin_ref)
                re, im = rotate(merged[ROWS * n : ROWS * n + ROWS], c, s)
                for top, tile in enumerate(by_top(re, im)):
                    hi_ref[2 * box + top], lo_ref[2 * box + top] = split_two(tile)

    @pl.loop(0, 2)
    def _(i):
        for sub in range(0, 16, SUB):
            pairs = [i * 16 + sub + n for n in range(SUB)]
            rows = [widen(*(load((hi_ref, lo_ref), 4 * q + 2 * c + h) for c in range(2))) for q in pairs for h in range(2)]
            merged = product(rows, k3_ref[1])
            for n in range(2 * SUB):
                low_bits = 2 * sub + n
                box = i * 32 + low_bits
                c, s = factors(1, box, 1, cos_ref, sin_ref)
                re, im = rotate(merged[ROWS * n : ROWS * n + ROWS], c, s)
                for top, tile in enumerate(by_top(re, im)):
                    outs[2 * top][box], outs[2 * top + 1][box] = split_two(tile)


def first_kernel(a_ref, k_ref, *refs):
    outs, (cos0_ref, sin0_ref, cos1_ref, sin1_ref), scratch = refs[:4], refs[4:8], refs[8:]
    build_tables(a_ref, ((cos0_ref, sin0_ref), (cos1_ref, sin1_ref)))
    early_steps(a_ref, ROWS + SLOPES, k_ref, cos0_ref, sin0_ref, outs, *scratch)


def second_kernel(a_ref, k_ref, cos_ref, sin_ref, *refs):
    outs, scratch, (held_ref, sems) = refs[:4], refs[4:-2], refs[-2:]

    def incoming(i):
        rows = pl.ds(pl.multiple_of(i * 64 * ROWS, 8), 64 * ROWS)
        return pltpu.make_async_copy(a_ref.at[rows], held_ref.at[rows], sems.at[i])

    for i in range(2):
        incoming(i).start()
    early_steps(held_ref, ROWS, k_ref, cos_ref, sin_ref, outs, *scratch, ready=lambda i: incoming(i).wait())


def late_kernel(
    x1, hi_ref, lo_ref, k_ref, e_ref, cos_ref, sin_ref, own_ref, send_ref, hi0_ref, lo0_ref, hi1_ref, lo1_ref, k3_ref, e3_ref
):
    fill_matrices(k_ref, k3_ref)
    high, low = split_two(e_ref[...])
    e3_ref[:, 0:256] = high
    e3_ref[:, 256:512] = high
    e3_ref[:, 512:768] = low
    states = ((hi0_ref, lo0_ref), (hi1_ref, lo1_ref))

    def finish(merged, n, step, box, direction):
        c, s = factors(step, insert_bit(box, 3, x1), direction, cos_ref, sin_ref)
        return rotate(merged[ROWS * n : ROWS * n + ROWS], c, s)

    def store(state, box, re, im):
        for top, tile in enumerate(by_top(re, im)):
            state[0][2 * box + top], state[1][2 * box + top] = split_two(tile)

    for sub in range(0, 32, 2 * SUB):
        boxes = range(sub, sub + 2 * SUB)
        rows = [widen(*(load((hi_ref, lo_ref), insert_bit(box, 3, c)) for c in range(2))) for box in boxes]
        merged = product(rows, k3_ref[0])
        for n, box in enumerate(boxes):
            store(states[0], box, *finish(merged, n, 2, box, 0))

    def middle(step, bit, direction, source, target):
        for sub in range(0, 16, SUB):
            pairs = [[insert_bit(sub + n, bit, c) for c in range(2)] for n in range(SUB)]
            rows = [widen(*(load(source, 2 * box + h) for box in pair)) for pair in pairs for h in range(2)]
            merged = product(rows, k3_ref[direction])
            for n in range(2 * SUB):
                box = pairs[n // 2][n % 2]
                store(target, box, *finish(merged, n, step, box, direction))

    @pl.loop(0, 2)
    def _(level):
        middle(2 * level + 3, level + 1, 1, states[0], states[1])
        middle(2 * level + 4, level + 3, 0, states[1], states[0])

    for sub in range(0, 16, SUB):
        boxes = [[2 * (sub + n) + c for c in range(2)] for n in range(SUB)]
        rows = [widen(*(load(states[0], 2 * box + h) for box in pair)) for pair in boxes for h in range(2)]
        merged = product(rows, k3_ref[1])
        rows = [None] * (2 * SUB)
        for n in range(2 * SUB):
            high, low = split_two(jnp.concatenate(finish(merged, n, 7, 2 * sub + n, 1), axis=1))
            rows[n // 4 * 4 + (0, 2, 1, 3)[n % 4]] = jnp.concatenate([high, low, high], axis=1)
        field = lax.dot_general(
            e3_ref[...], jnp.concatenate(rows, axis=0), (((1,), (1,)), ((), ())), preferred_element_type=F32
        )
        own_ref[:, 64 * sub : 64 * sub + 64 * SUB] = field[0:64]
        send_ref[:, 64 * sub : 64 * sub + 64 * SUB] = field[64:128]


VMEM = pl.BlockSpec(memory_space=pltpu.VMEM)
TABLE = jax.ShapeDtypeStruct((32, ROWS, 128), F32)
HALF = jax.ShapeDtypeStruct((64, ROWS, 128), BF16)
FIELD = jax.ShapeDtypeStruct((64, 1024), F32)
MATRICES = pltpu.VMEM((2, 768, 256), BF16)


def cost(flops):
    return pl.CostEstimate(flops=flops, bytes_accessed=4 << 20, transcendentals=0)


def first_part(arrived, k):
    return pl.pallas_call(
        first_kernel,
        out_shape=[HALF] * 4 + [TABLE] * 4,
        in_specs=[VMEM, VMEM],
        out_specs=[VMEM] * 8,
        scratch_shapes=[pltpu.VMEM((128, ROWS, 128), BF16)] * 2 + [MATRICES],
        compiler_params=pltpu.CompilerParams(vmem_limit_bytes=MAIN_VMEM),
        cost_estimate=cost(4_000_000_000),
    )(arrived, k)


def second_part(arrived, k, cos, sin):
    return pl.pallas_call(
        second_kernel,
        out_shape=[HALF] * 4,
        in_specs=[pl.BlockSpec(memory_space=pl.ANY)] + [VMEM] * 3,
        out_specs=[VMEM] * 4,
        scratch_shapes=[pltpu.VMEM((128, ROWS, 128), BF16)] * 2
        + [MATRICES, pltpu.VMEM((128 * ROWS, 128), F32), pltpu.SemaphoreType.DMA((2,))],
        compiler_params=pltpu.CompilerParams(vmem_limit_bytes=MAIN_VMEM),
        cost_estimate=cost(3_000_000_000),
    )(arrived, k, cos, sin)


def late_part(x1, high, low, k, e, cos, sin):
    return pl.pallas_call(
        functools.partial(late_kernel, x1),
        out_shape=[FIELD, FIELD],
        in_specs=[VMEM] * 6,
        out_specs=[VMEM] * 2,
        scratch_shapes=[pltpu.VMEM((64, ROWS, 128), BF16)] * 4 + [MATRICES, pltpu.VMEM((128, 768), BF16)],
        compiler_params=pltpu.CompilerParams(vmem_limit_bytes=MAIN_VMEM),
        cost_estimate=cost(5_000_000_000),
    )(high, low, k, e, cos, sin)


def join_kernel(place, w_ref, own_ref, got_ref, *rest):
    out_ref, held_ref, sems = rest[-3:]
    first = w_ref[0] == 0
    lane = lax.broadcasted_iota(jnp.int32, (64, 128), 1)
    even = lane // 32 % 2 == 0
    copies = []
    for box in range(4):
        for y2 in range(2):
            lanes = slice(256 * box + 128 * y2, 256 * box + 128 * y2 + 128)
            own = own_ref[:, lanes]
            got = got_ref[:, lanes]
            a = jnp.where(first, own, got)
            b = jnp.where(first, got, own)
            held_ref[box, :, 256 * y2 : 256 * y2 + 128] = jnp.where(even, a, pltpu.roll(b, 32, 1))
            held_ref[box, :, 256 * y2 + 128 : 256 * y2 + 256] = jnp.where(even, pltpu.roll(a, 96, 1), b)
        at = (4 * box + place) * 512
        copies.append(pltpu.make_async_copy(held_ref.at[box], out_ref.at[:, at : at + 512], sems.at[box]))
        copies[-1].start()
    for copy in copies:
        copy.wait()


def join(w, own, got, place, out):
    more = [] if out is None else [out]
    anywhere = pl.BlockSpec(memory_space=pl.ANY)
    return pl.pallas_call(
        functools.partial(join_kernel, place),
        out_shape=jax.ShapeDtypeStruct((64, 8192), F32),
        in_specs=[pl.BlockSpec(memory_space=pltpu.SMEM), VMEM, VMEM] + [anywhere] * len(more),
        out_specs=anywhere,
        scratch_shapes=[pltpu.VMEM((4, 64, 512), F32), pltpu.SemaphoreType.DMA((4,))],
        input_output_aliases={3: 0} if more else {},
        compiler_params=pltpu.CompilerParams(vmem_limit_bytes=MAIN_VMEM),
        cost_estimate=pl.CostEstimate(flops=0, bytes_accessed=1 << 20, transcendentals=0),
    )(w, own, got, *more)


def merge_matrices(interp_matrix):
    re = jnp.transpose(interp_matrix[:, 0], (0, 3, 4, 1, 2)).reshape(2, 2, 64, 128)
    im = jnp.transpose(interp_matrix[:, 1], (0, 3, 4, 1, 2)).reshape(2, 2, 64, 128)
    from_re = jnp.concatenate([re, im], axis=3)
    from_im = jnp.concatenate([-im, re], axis=3)
    return jnp.stack([from_re, from_im], axis=2).reshape(2, 256, 256)


def evaluation_matrix(evaluation, w):
    zero = jnp.zeros((64, 64), F32)
    re, im = evaluation[0], -evaluation[1]
    low = jnp.concatenate([re, zero, im, zero], axis=1)
    high = jnp.concatenate([zero, re, zero, im], axis=1)
    return jnp.where(w == 0, jnp.concatenate([low, high], axis=0), jnp.concatenate([high, low], axis=0))


def shards(weights, phase_slope, interp_matrix, evaluation):
    w = lax.axis_index("bx") >> 3
    w_one = w.astype(jnp.int32).reshape(1)
    planes = weights.reshape(128, 8192)
    k = merge_matrices(interp_matrix)
    e = evaluation_matrix(evaluation, w)

    def spread(packed):
        return lax.all_to_all(packed.reshape(128, 1, -1), AXES, split_axis=0, concat_axis=0, tiled=True).reshape(-1, 128)

    def swap(field):
        return lax.ppermute(field, "bx", [(i, i ^ 8) for i in range(16)])

    arrived0 = spread(pack(planes, phase_slope.reshape(8, 1, 8192), 0))
    arrived1 = spread(pack(planes, None, 1))
    out = None
    for top in range(2):
        if top == 0:
            *halves, cos, sin, cos1, sin1 = first_part(arrived0, k)
        else:
            cos, sin = cos1, sin1
            halves = second_part(arrived1, k, cos, sin)
        for x1 in range(2):
            own, send = late_part(x1, halves[2 * x1], halves[2 * x1 + 1], k, e, cos, sin)
            out = join(w_one, own, swap(send), 2 * x1 + top, out)
    return out[None, None]


def solution(mesh):
    in_specs = (P("bx", "by", None, None, None), P(None, "bx", "by", None), P(), P())
    out_specs = P("bx", "by", None, None)
    return jax.shard_map(shards, mesh=mesh, in_specs=in_specs, out_specs=out_specs, check_vma=False)
```

```python
import functools

import jax
import jax.numpy as jnp
import numpy as np
from jax import lax
from jax.experimental import pallas as pl
from jax.experimental.pallas import tpu as pltpu
from jax.sharding import PartitionSpec as P

PACK_VMEM = 60 << 20
MAIN_VMEM = 24 << 20
AXES = ("bx", "by")
ROWS = 32
SLOPES = 4
NODES = [float(np.cos(np.pi * (2 * m + 1) / 16)) for m in range(4)]
F32 = jnp.float32
BF16 = jnp.bfloat16


def split_two(value):
    high = value.astype(BF16)
    low = (value - high.astype(F32)).astype(BF16)
    return high, low


def pack_kernel(top, rows, w_ref, *refs):
    p_ref = refs[0] if rows > ROWS else None
    out_ref, held_ref, made_ref, p_held_ref, in_sems, out_sems = refs[-6:]
    pieces, _, lanes = held_ref.shape
    half = pieces * lanes
    tall = lanes // 64 * rows

    def incoming(n):
        at = pl.ds(pl.multiple_of(top * half + n * lanes, 128), lanes)
        return pltpu.make_async_copy(w_ref.at[:, at], held_ref.at[n], in_sems.at[n])

    def outgoing(n, w):
        at = pl.ds(pl.multiple_of(n * tall, 8), tall)
        return pltpu.make_async_copy(made_ref.at[w, at], out_ref.at[w, at], out_sems.at[n, w])

    more = []
    if p_ref is not None:
        more = [pltpu.make_async_copy(p_ref, p_held_ref, in_sems.at[pieces])]
        more[0].start()
    for n in range(pieces):
        incoming(n).start()
    if p_ref is not None:
        more[0].wait()

        @pl.loop(0, pieces)
        def _(n):
            first = pl.multiple_of(n * tall, 8)
            p0 = p_held_ref[:, 0, pl.ds(pl.multiple_of(n * lanes, 128), lanes)]
            p1 = p_held_ref[:, 0, pl.ds(pl.multiple_of(half + n * lanes, 128), lanes)]
            for b in range(lanes // 64):
                for w in range(2):
                    at = slice(64 * b + 32 * w, 64 * b + 32 * w + 32)
                    parts = [p0[0:4, at], p1[0:4, at], p0[4:8, at], p1[4:8, at]]
                    to = first + (b * rows + ROWS)
                    made_ref[w, pl.ds(to, SLOPES), :] = jnp.concatenate(parts, axis=1)

    @pl.loop(0, pieces)
    def _(n):
        incoming(n).wait()
        first = pl.multiple_of(n * tall, 8)
        for pair in range(lanes // 128):
            turned = held_ref[n, :, pair * 128 : pair * 128 + 128].T
            for b in range(2):
                for w in range(2):
                    at = 64 * b + 32 * w
                    made_ref[w, pl.ds(first + (2 * pair + b) * rows, ROWS), :] = turned[at : at + 32]
        for w in range(2):
            outgoing(n, w).start()

    @pl.loop(0, pieces)
    def _(n):
        for w in range(2):
            outgoing(n, w).wait()


def pack(weights, slopes, top):
    pieces, lanes = 4, 1024
    rows = ROWS if slopes is None else ROWS + SLOPES
    more = [] if slopes is None else [slopes]
    anywhere = pl.BlockSpec(memory_space=pl.ANY)
    return pl.pallas_call(
        functools.partial(pack_kernel, top, rows),
        out_shape=jax.ShapeDtypeStruct((2, 64 * rows, 128), F32),
        in_specs=[anywhere] * (1 + len(more)),
        out_specs=anywhere,
        scratch_shapes=[
            pltpu.VMEM((pieces, 128, lanes), F32),
            pltpu.VMEM((2, 64 * rows, 128), F32),
            pltpu.VMEM((8, 1, 8192), F32),
            pltpu.SemaphoreType.DMA((pieces + 1,)),
            pltpu.SemaphoreType.DMA((pieces, 2)),
        ],
        compiler_params=pltpu.CompilerParams(vmem_limit_bytes=PACK_VMEM),
        cost_estimate=pl.CostEstimate(flops=0, bytes_accessed=5 << 20, transcendentals=0),
    )(weights, *more)


def sincos(angle):
    h = angle * 0.5
    q = h * h
    s = q * (-1 / 39916800) + 1 / 362880
    s = s * q - 1 / 5040
    s = s * q + 1 / 120
    s = s * q - 1 / 6
    s = (s * q + 1.0) * h
    c = q * (1 / 479001600) - 1 / 3628800
    c = c * q + 1 / 40320
    c = c * q - 1 / 720
    c = c * q + 1 / 24
    c = c * q - 0.5
    c = c * q + 1.0
    return 2.0 * s * c, 1.0 - 2.0 * s * s


def lane_gather(value, index):
    return jnp.take_along_axis(value, index, axis=1, mode="promise_in_bounds")


def build_tables(a_ref, tables):
    lane = lax.broadcasted_iota(jnp.int32, (ROWS, 128), 1)
    m = lane % 4
    node = jnp.where(m == 0, NODES[0], jnp.where(m == 1, NODES[1], jnp.where(m == 2, NODES[2], NODES[3])))
    second = lane // 4 % 2 == 1
    g = lane // 8

    @pl.loop(0, SLOPES)
    def _(row):
        turned = a_ref[pl.ds(ROWS + row, 128, stride=ROWS + SLOPES), :].T
        for late in range(2):
            t0 = turned[64 * late : 64 * late + 32]
            t1 = turned[64 * late + 32 : 64 * late + 64]
            for tile in range(4):
                for h, (cos_ref, sin_ref) in enumerate(tables):
                    index = ((2 * (2 * tile + g // 8) + h) * 8) + g % 8
                    slope = jnp.where(second, lane_gather(t1, index), lane_gather(t0, index))
                    s, c = sincos(slope * node)
                    at = (row + SLOPES * late) * 4 + tile
                    cos_ref[at] = c
                    sin_ref[at] = s


def factors(step, box, direction, flip, cos_ref, sin_ref):
    lane = lax.broadcasted_iota(jnp.int32, (ROWS, 128), 1)
    p = lane % 64
    m = p // 8 if direction == 0 else p % 8
    index = (lane // 64 + flip) % 2 * 4 + jnp.where(m < 4, m, 7 - m) + (box % 16) * 8
    tile = step * 4 + box // 16
    c = lane_gather(cos_ref[tile], index)
    s = lane_gather(sin_ref[tile], index)
    return c, jnp.where(m < 4, s, -s)


def rotate(merged, c, s):
    re = merged[:, :128]
    im = merged[:, 128:]
    return re * c - im * s, re * s + im * c


def insert_bit(q, bit, value):
    return ((q >> bit) << (bit + 1)) | (value << bit) | (q & ((1 << bit) - 1))


SUB = 8


def fill_matrices(k_ref, e_ref, k3_ref, k0_ref, e3_ref):
    def fill(to, value):
        high, low = split_two(value)
        to[0:256] = high
        to[256:512] = high
        to[512:768] = low

    for d in range(2):
        for flip in range(2):
            value = k_ref[d]
            if flip:
                value = jnp.concatenate([pltpu.roll(value[:, 128 * n : 128 * n + 128], 64, 1) for n in range(2)], axis=1)
            if d == 0:
                fill(k0_ref.at[flip], value)
            for h in range(2):
                parts = [value[128 * c + 64 * part : 128 * c + 64 * part + 64] for part in range(2) for c in (h, 1 - h)]
                fill(k3_ref.at[d, h, flip], jnp.concatenate(parts, axis=0))
    high, low = split_two(e_ref[...])
    e3_ref[:, 0:256] = high
    e3_ref[:, 256:512] = high
    e3_ref[:, 512:768] = low


def product(rows, matrix):
    return jnp.dot(jnp.concatenate(rows, axis=0), matrix, preferred_element_type=F32)


def children(state, first, second):
    lower = lax.broadcasted_iota(jnp.int32, (ROWS, 128), 1).astype(F32).astype(BF16) < 64
    high_re, high_im, low_re, low_im = (jnp.where(lower, ref[first], ref[second]) for ref in state)
    return jnp.concatenate([high_re, high_im, low_re, low_im, high_re, high_im], axis=1)


def store(state, box, re, im):
    state[0][box], state[2][box] = split_two(re)
    state[1][box], state[3][box] = split_two(im)


def finish(merged, n, step, box, direction, flip, tables):
    c, s = factors(step, box, direction, flip, *tables)
    return rotate(merged[ROWS * n : ROWS * n + ROWS], c, s)


def early_steps(a_ref, stride, tables, middle, target, k3_ref, k0_ref, ready=lambda i: None):
    def arrived(pair, odd):
        at = pl.multiple_of(pair * 2 * stride, 8)
        if stride % 8 == 0:
            return a_ref[pl.ds(at + odd * stride, ROWS), :]
        shift = odd * stride % 8
        return a_ref[pl.ds(at + (odd * stride - shift), ROWS + 2 * shift), :][shift : shift + ROWS]

    @pl.loop(0, 2)
    def _(i):
        ready(i)
        for sub in range(0, 32, 2 * SUB):
            for y0 in range(2):
                boxes = [i * 32 + (sub + 2 * n + y0) for n in range(SUB)]
                rows = []
                for n in range(SUB):
                    pair = i * 32 + (sub // 8 * 8 + n // 4 * 8 + n % 4)
                    parts = [split_two(arrived(pair + 4 * c, y0)) for c in range(2)]
                    highs = [p[0] for p in parts]
                    lows = [p[1] for p in parts]
                    rows.append(jnp.concatenate(highs + lows + highs, axis=1))
                merged = product(rows, k0_ref[y0])
                for n, box in enumerate(boxes):
                    store(middle, box, *finish(merged, n, 0, box, 0, y0, tables))

    @pl.loop(0, 2)
    def _(i):
        for h in range(2):
            for x1 in range(2):
                pairs = [i * 32 + (n // 4 * 16 + x1 * 8 + n % 4 * 2) for n in range(SUB)]
                merged = product([children(middle, q + h, q + 1 - h) for q in pairs], k3_ref[1, h, x1])
                for n in range(SUB):
                    store(target, pairs[n] + h, *finish(merged, n, 1, pairs[n] + h, 1, x1, tables))


def first_kernel(a_ref, k_ref, e_ref, *refs):
    target, tables, (k3_ref, e3_ref, k0_ref), middle = refs[:4], refs[4:8], refs[8:11], refs[11:]
    build_tables(a_ref, (tables[:2], tables[2:]))
    fill_matrices(k_ref, e_ref, k3_ref, k0_ref, e3_ref)
    early_steps(a_ref, ROWS + SLOPES, tables[:2], middle, target, k3_ref, k0_ref)


def second_kernel(a_ref, k_ref, e_ref, cos_ref, sin_ref, *refs):
    target, (k3_ref, e3_ref, k0_ref), middle, (held_ref, sems) = refs[:4], refs[4:7], refs[7:11], refs[11:]

    def incoming(i):
        rows = pl.ds(pl.multiple_of(i * 64 * ROWS, 8), 64 * ROWS)
        return pltpu.make_async_copy(a_ref.at[rows], held_ref.at[rows], sems.at[i])

    for i in range(2):
        incoming(i).start()
    fill_matrices(k_ref, e_ref, k3_ref, k0_ref, e3_ref)
    early_steps(held_ref, ROWS, (cos_ref, sin_ref), middle, target, k3_ref, k0_ref, lambda i: incoming(i).wait())


def late_kernel(x1, *refs):
    source, (k3_ref, e3_ref), tables, (own_ref, send_ref) = refs[:4], refs[4:6], refs[6:8], refs[8:10]
    states = (refs[10:14], refs[14:18])

    def done(merged, n, step, box, direction, flip):
        return finish(merged, n, step, insert_bit(box, 3, x1), direction, flip, tables)

    for y1 in range(2):
        for half in range(2):
            boxes = [half * 16 + (n // 2 * 4 + y1 * 2 + n % 2) for n in range(SUB)]
            rows = [children(source, insert_bit(box, 3, x1), insert_bit(box, 3, 1 - x1)) for box in boxes]
            merged = product(rows, k3_ref[0, x1, y1])
            for n, box in enumerate(boxes):
                store(states[0], box, *done(merged, n, 2, box, 0, y1))

    def middle(step, bit, after, direction, source, target):
        for h in range(2):
            for flip in range(2):
                if direction == 0:
                    pairs = [[insert_bit(insert_bit(n, after, flip), bit, c) for c in (h, 1 - h)] for n in range(SUB)]
                else:
                    pairs = [[insert_bit(insert_bit(n, bit, c), after, flip) for c in (h, 1 - h)] for n in range(SUB)]
                merged = product([children(source, *pair) for pair in pairs], k3_ref[direction, h, flip])
                for n, (box, _) in enumerate(pairs):
                    store(target, box, *done(merged, n, step, box, direction, flip))

    @pl.loop(0, 2)
    def _(level):
        middle(2 * level + 3, level + 1, level + 3, 1, states[0], states[1])
        middle(2 * level + 4, level + 3, jnp.where(level == 0, 2, 0), 0, states[1], states[0])

    for quarter in range(2):
        tiles = {}
        for h in range(2):
            boxes = [quarter * 16 + 2 * n for n in range(SUB)]
            merged = product([children(states[0], box + h, box + 1 - h) for box in boxes], k3_ref[1, h, 0])
            for n, box in enumerate(boxes):
                high, low = split_two(jnp.concatenate(done(merged, n, 7, box + h, 1, 0), axis=1))
                tiles[2 * n + h] = jnp.concatenate([high, low, high], axis=1)
        for part in range(2):
            rows = [tiles[8 * part + n // 4 * 4 + (0, 2, 1, 3)[n % 4]] for n in range(8)]
            field = lax.dot_general(
                e3_ref[...], jnp.concatenate(rows, axis=0), (((1,), (1,)), ((), ())), preferred_element_type=F32
            )
            at = 512 * quarter + 256 * part
            own_ref[:, at : at + 256] = field[0:64]
            send_ref[:, at : at + 256] = field[64:128]


VMEM = pl.BlockSpec(memory_space=pltpu.VMEM)
TABLE = jax.ShapeDtypeStruct((32, ROWS, 128), F32)
STATE = jax.ShapeDtypeStruct((64, ROWS, 128), BF16)
FIELD = jax.ShapeDtypeStruct((64, 1024), F32)
K3 = jax.ShapeDtypeStruct((2, 2, 2, 768, 256), BF16)
K0 = pltpu.VMEM((2, 768, 256), BF16)
E3 = jax.ShapeDtypeStruct((128, 768), BF16)


def cost(flops):
    return pl.CostEstimate(flops=flops, bytes_accessed=4 << 20, transcendentals=0)


def first_part(arrived, k, e):
    return pl.pallas_call(
        first_kernel,
        out_shape=[STATE] * 4 + [TABLE] * 4 + [K3, E3],
        in_specs=[VMEM] * 3,
        out_specs=[VMEM] * 10,
        scratch_shapes=[K0] + [pltpu.VMEM(STATE.shape, BF16)] * 4,
        compiler_params=pltpu.CompilerParams(vmem_limit_bytes=MAIN_VMEM),
        cost_estimate=cost(4_000_000_000),
    )(arrived, k, e)


def second_part(arrived, k, e, cos, sin):
    return pl.pallas_call(
        second_kernel,
        out_shape=[STATE] * 4 + [K3, E3],
        in_specs=[pl.BlockSpec(memory_space=pl.ANY)] + [VMEM] * 4,
        out_specs=[VMEM] * 6,
        scratch_shapes=[K0]
        + [pltpu.VMEM(STATE.shape, BF16)] * 4
        + [pltpu.VMEM((128 * ROWS, 128), F32), pltpu.SemaphoreType.DMA((2,))],
        compiler_params=pltpu.CompilerParams(vmem_limit_bytes=MAIN_VMEM),
        cost_estimate=cost(3_000_000_000),
    )(arrived, k, e, cos, sin)


def late_part(x1, state, k3, e3, cos, sin):
    return pl.pallas_call(
        functools.partial(late_kernel, x1),
        out_shape=[FIELD, FIELD],
        in_specs=[VMEM] * 8,
        out_specs=[VMEM] * 2,
        scratch_shapes=[pltpu.VMEM((32, ROWS, 128), BF16)] * 8,
        compiler_params=pltpu.CompilerParams(vmem_limit_bytes=MAIN_VMEM),
        cost_estimate=cost(5_000_000_000),
    )(*state, k3, e3, cos, sin)


def join_kernel(place, w_ref, own_ref, got_ref, *rest):
    out_ref, held_ref, sems = rest[-3:]
    first = w_ref[0] == 0
    lane = lax.broadcasted_iota(jnp.int32, (64, 128), 1)
    even = lane // 32 % 2 == 0
    copies = []
    for box in range(4):
        for y2 in range(2):
            lanes = slice(256 * box + 128 * y2, 256 * box + 128 * y2 + 128)
            own = own_ref[:, lanes]
            got = got_ref[:, lanes]
            a = jnp.where(first, own, got)
            b = jnp.where(first, got, own)
            held_ref[box, :, 256 * y2 : 256 * y2 + 128] = jnp.where(even, a, pltpu.roll(b, 32, 1))
            held_ref[box, :, 256 * y2 + 128 : 256 * y2 + 256] = jnp.where(even, pltpu.roll(a, 96, 1), b)
        at = (4 * box + place) * 512
        copies.append(pltpu.make_async_copy(held_ref.at[box], out_ref.at[:, at : at + 512], sems.at[box]))
        copies[-1].start()
    for copy in copies:
        copy.wait()


def join(w, own, got, place, out):
    more = [] if out is None else [out]
    anywhere = pl.BlockSpec(memory_space=pl.ANY)
    return pl.pallas_call(
        functools.partial(join_kernel, place),
        out_shape=jax.ShapeDtypeStruct((64, 8192), F32),
        in_specs=[pl.BlockSpec(memory_space=pltpu.SMEM), VMEM, VMEM] + [anywhere] * len(more),
        out_specs=anywhere,
        scratch_shapes=[pltpu.VMEM((4, 64, 512), F32), pltpu.SemaphoreType.DMA((4,))],
        input_output_aliases={3: 0} if more else {},
        compiler_params=pltpu.CompilerParams(vmem_limit_bytes=MAIN_VMEM),
        cost_estimate=pl.CostEstimate(flops=0, bytes_accessed=1 << 20, transcendentals=0),
    )(w, own, got, *more)


def merge_matrices(interp_matrix):
    re = jnp.transpose(interp_matrix[:, 0], (0, 3, 4, 1, 2)).reshape(2, 2, 64, 128)
    im = jnp.transpose(interp_matrix[:, 1], (0, 3, 4, 1, 2)).reshape(2, 2, 64, 128)
    from_re = jnp.concatenate([re, im], axis=3)
    from_im = jnp.concatenate([-im, re], axis=3)
    return jnp.stack([from_re, from_im], axis=2).reshape(2, 256, 256)


def evaluation_matrix(evaluation, w):
    zero = jnp.zeros((64, 64), F32)
    re, im = evaluation[0], -evaluation[1]
    low = jnp.concatenate([re, zero, im, zero], axis=1)
    high = jnp.concatenate([zero, re, zero, im], axis=1)
    return jnp.where(w == 0, jnp.concatenate([low, high], axis=0), jnp.concatenate([high, low], axis=0))


def shards(weights, phase_slope, interp_matrix, evaluation):
    w = lax.axis_index("bx") >> 3
    w_one = w.astype(jnp.int32).reshape(1)
    planes = weights.reshape(128, 8192)
    k = merge_matrices(interp_matrix)
    e = evaluation_matrix(evaluation, w)

    def spread(packed):
        return lax.all_to_all(packed.reshape(128, 1, -1), AXES, split_axis=0, concat_axis=0, tiled=True).reshape(-1, 128)

    def swap(field):
        return lax.ppermute(field, "bx", [(i, i ^ 8) for i in range(16)])

    arrived0 = spread(pack(planes, phase_slope.reshape(8, 1, 8192), 0))
    arrived1 = spread(pack(planes, None, 1))
    *first, cos0, sin0, cos1, sin1, k3, e3 = first_part(arrived0, k, e)
    fields = [late_part(x1, first, k3, e3, cos0, sin0) for x1 in range(2)]
    *second, k3, e3 = second_part(arrived1, k, e, cos1, sin1)
    fields += [late_part(x1, second, k3, e3, cos1, sin1) for x1 in range(2)]
    out = None
    for n, (own, send) in enumerate(fields):
        out = join(w_one, own, swap(send), n % 2 * 2 + n // 2, out)
    return out[None, None]


def solution(mesh):
    in_specs = (P("bx", "by", None, None, None), P(None, "bx", "by", None), P(), P())
    out_specs = P("bx", "by", None, None)
    return jax.shard_map(shards, mesh=mesh, in_specs=in_specs, out_specs=out_specs, check_vma=False)
```

```python
import functools

import jax
import jax.numpy as jnp
import numpy as np
from jax import lax
from jax.experimental import pallas as pl
from jax.experimental.pallas import tpu as pltpu
from jax.sharding import PartitionSpec as P

PACK_VMEM = 60 << 20
MAIN_VMEM = 24 << 20
AXES = ("bx", "by")
ROWS = 32
SLOPES = 4
NODES = [float(np.cos(np.pi * (2 * m + 1) / 16)) for m in range(4)]
F32 = jnp.float32
BF16 = jnp.bfloat16


def split_two(value):
    high = value.astype(BF16)
    low = (value - high.astype(F32)).astype(BF16)
    return high, low


def pack_kernel(top, rows, w_ref, *refs):
    p_ref = refs[0] if rows > ROWS else None
    out_ref, held_ref, made_ref, p_held_ref, in_sems, out_sems = refs[-6:]
    pieces, _, lanes = held_ref.shape
    half = pieces * lanes
    tall = lanes // 64 * rows

    def incoming(n):
        at = pl.ds(pl.multiple_of(top * half + n * lanes, 128), lanes)
        return pltpu.make_async_copy(w_ref.at[:, at], held_ref.at[n], in_sems.at[n])

    def outgoing(n, w):
        at = pl.ds(pl.multiple_of(n * tall, 8), tall)
        return pltpu.make_async_copy(made_ref.at[w, at], out_ref.at[w, at], out_sems.at[n, w])

    more = []
    if p_ref is not None:
        more = [pltpu.make_async_copy(p_ref, p_held_ref, in_sems.at[pieces])]
        more[0].start()
    for n in range(pieces):
        incoming(n).start()
    if p_ref is not None:
        more[0].wait()

        @pl.loop(0, pieces)
        def _(n):
            first = pl.multiple_of(n * tall, 8)
            p0 = p_held_ref[:, 0, pl.ds(pl.multiple_of(n * lanes, 128), lanes)]
            p1 = p_held_ref[:, 0, pl.ds(pl.multiple_of(half + n * lanes, 128), lanes)]
            for b in range(lanes // 64):
                for w in range(2):
                    at = slice(64 * b + 32 * w, 64 * b + 32 * w + 32)
                    parts = [p0[0:4, at], p1[0:4, at], p0[4:8, at], p1[4:8, at]]
                    to = first + (b * rows + ROWS)
                    made_ref[w, pl.ds(to, SLOPES), :] = jnp.concatenate(parts, axis=1)

    @pl.loop(0, pieces)
    def _(n):
        incoming(n).wait()
        first = pl.multiple_of(n * tall, 8)
        for pair in range(lanes // 128):
            turned = held_ref[n, :, pair * 128 : pair * 128 + 128].T
            for b in range(2):
                for w in range(2):
                    at = 64 * b + 32 * w
                    made_ref[w, pl.ds(first + (2 * pair + b) * rows, ROWS), :] = turned[at : at + 32]
        for w in range(2):
            outgoing(n, w).start()

    @pl.loop(0, pieces)
    def _(n):
        for w in range(2):
            outgoing(n, w).wait()


def pack(weights, slopes, top):
    pieces, lanes = 4, 1024
    rows = ROWS if slopes is None else ROWS + SLOPES
    more = [] if slopes is None else [slopes]
    anywhere = pl.BlockSpec(memory_space=pl.ANY)
    return pl.pallas_call(
        functools.partial(pack_kernel, top, rows),
        out_shape=jax.ShapeDtypeStruct((2, 64 * rows, 128), F32),
        in_specs=[anywhere] * (1 + len(more)),
        out_specs=anywhere,
        scratch_shapes=[
            pltpu.VMEM((pieces, 128, lanes), F32),
            pltpu.VMEM((2, 64 * rows, 128), F32),
            pltpu.VMEM((8, 1, 8192), F32),
            pltpu.SemaphoreType.DMA((pieces + 1,)),
            pltpu.SemaphoreType.DMA((pieces, 2)),
        ],
        compiler_params=pltpu.CompilerParams(vmem_limit_bytes=PACK_VMEM),
        cost_estimate=pl.CostEstimate(flops=0, bytes_accessed=5 << 20, transcendentals=0),
    )(weights, *more)


def sincos(angle):
    h = angle * 0.5
    q = h * h
    s = q * (-1 / 39916800) + 1 / 362880
    s = s * q - 1 / 5040
    s = s * q + 1 / 120
    s = s * q - 1 / 6
    s = (s * q + 1.0) * h
    c = q * (1 / 479001600) - 1 / 3628800
    c = c * q + 1 / 40320
    c = c * q - 1 / 720
    c = c * q + 1 / 24
    c = c * q - 0.5
    c = c * q + 1.0
    return 2.0 * s * c, 1.0 - 2.0 * s * s


def lane_gather(value, index):
    return jnp.take_along_axis(value, index, axis=1, mode="promise_in_bounds")


def build_tables(a_ref, tables):
    lane = lax.broadcasted_iota(jnp.int32, (ROWS, 128), 1)
    m = lane % 4
    node = jnp.where(m == 0, NODES[0], jnp.where(m == 1, NODES[1], jnp.where(m == 2, NODES[2], NODES[3])))
    second = lane // 4 % 2 == 1
    g = lane // 8

    @pl.loop(0, SLOPES)
    def _(row):
        turned = a_ref[pl.ds(ROWS + row, 128, stride=ROWS + SLOPES), :].T
        for late in range(2):
            t0 = turned[64 * late : 64 * late + 32]
            t1 = turned[64 * late + 32 : 64 * late + 64]
            for tile in range(4):
                for h, (cos_ref, sin_ref) in enumerate(tables):
                    index = ((2 * (2 * tile + g // 8) + h) * 8) + g % 8
                    slope = jnp.where(second, lane_gather(t1, index), lane_gather(t0, index))
                    s, c = sincos(slope * node)
                    at = (row + SLOPES * late) * 4 + tile
                    cos_ref[at] = c
                    sin_ref[at] = s


def factors(step, box, direction, flip, cos_ref, sin_ref):
    lane = lax.broadcasted_iota(jnp.int32, (ROWS, 128), 1)
    p = lane % 64
    m = p // 8 if direction == 0 else p % 8
    index = (lane // 64 + flip) % 2 * 4 + jnp.where(m < 4, m, 7 - m) + (box % 16) * 8
    tile = step * 4 + box // 16
    c = lane_gather(cos_ref[tile], index)
    s = lane_gather(sin_ref[tile], index)
    return c, jnp.where(m < 4, s, -s)


def rotate(merged, c, s):
    re = merged[:, :128]
    im = merged[:, 128:]
    return re * c - im * s, re * s + im * c


def insert_bit(q, bit, value):
    return ((q >> bit) << (bit + 1)) | (value << bit) | (q & ((1 << bit) - 1))


SUB = 8


def fill_matrices(k_ref, e_ref, k3_ref, k0_ref, e3_ref):
    def fill(to, value):
        high, low = split_two(value)
        to[0:256] = high
        to[256:512] = high
        to[512:768] = low

    for d in range(2):
        for flip in range(2):
            value = k_ref[d]
            if flip:
                value = jnp.concatenate([pltpu.roll(value[:, 128 * n : 128 * n + 128], 64, 1) for n in range(2)], axis=1)
            if d == 0:
                fill(k0_ref.at[flip], value)
            for h in range(2):
                parts = [value[128 * c + 64 * part : 128 * c + 64 * part + 64] for part in range(2) for c in (h, 1 - h)]
                fill(k3_ref.at[d, h, flip], jnp.concatenate(parts, axis=0))
    high, low = split_two(e_ref[...])
    e3_ref[:, 0:256] = high
    e3_ref[:, 256:512] = high
    e3_ref[:, 512:768] = low


def product(rows, matrix):
    return jnp.dot(jnp.concatenate(rows, axis=0), matrix, preferred_element_type=F32)


def children(state, first, second):
    lower = lax.broadcasted_iota(jnp.int32, (ROWS, 128), 1).astype(F32).astype(BF16) < 64
    high_re, high_im, low_re, low_im = (jnp.where(lower, ref[first], ref[second]) for ref in state)
    return jnp.concatenate([high_re, high_im, low_re, low_im, high_re, high_im], axis=1)


def store(state, box, re, im):
    state[0][box], state[2][box] = split_two(re)
    state[1][box], state[3][box] = split_two(im)


def finish(merged, n, step, box, direction, flip, tables):
    c, s = factors(step, box, direction, flip, *tables)
    return rotate(merged[ROWS * n : ROWS * n + ROWS], c, s)


def early_steps(a_ref, stride, tables, middle, target, k3_ref, k0_ref, ready=lambda i: None):
    def arrived(pair, odd):
        at = (2 * pair + odd) * stride
        return a_ref[at : at + ROWS, :]

    for i in range(2):
        ready(i)
        for sub in range(0, 32, 2 * SUB):
            for y0 in range(2):
                boxes = [i * 32 + (sub + 2 * n + y0) for n in range(SUB)]
                rows = []
                for n in range(SUB):
                    pair = i * 32 + (sub // 8 * 8 + n // 4 * 8 + n % 4)
                    parts = [split_two(arrived(pair + 4 * c, y0)) for c in range(2)]
                    highs = [p[0] for p in parts]
                    lows = [p[1] for p in parts]
                    rows.append(jnp.concatenate(highs + lows + highs, axis=1))
                merged = product(rows, k0_ref[y0])
                for n, box in enumerate(boxes):
                    store(middle, box, *finish(merged, n, 0, box, 0, y0, tables))

    for i in range(2):
        for h in range(2):
            for x1 in range(2):
                pairs = [i * 32 + (n // 4 * 16 + x1 * 8 + n % 4 * 2) for n in range(SUB)]
                merged = product([children(middle, q + h, q + 1 - h) for q in pairs], k3_ref[1, h, x1])
                for n in range(SUB):
                    store(target, pairs[n] + h, *finish(merged, n, 1, pairs[n] + h, 1, x1, tables))


def first_kernel(a_ref, k_ref, e_ref, *refs):
    target, tables, (k3_ref, e3_ref, k0_ref), middle = refs[:4], refs[4:8], refs[8:11], refs[11:]
    build_tables(a_ref, (tables[:2], tables[2:]))
    fill_matrices(k_ref, e_ref, k3_ref, k0_ref, e3_ref)
    early_steps(a_ref, ROWS + SLOPES, tables[:2], middle, target, k3_ref, k0_ref)


def second_kernel(a_ref, k_ref, e_ref, cos_ref, sin_ref, *refs):
    target, (k3_ref, e3_ref, k0_ref), middle, (held_ref, sems) = refs[:4], refs[4:7], refs[7:11], refs[11:]

    def incoming(i):
        rows = pl.ds(pl.multiple_of(i * 64 * ROWS, 8), 64 * ROWS)
        return pltpu.make_async_copy(a_ref.at[rows], held_ref.at[rows], sems.at[i])

    for i in range(2):
        incoming(i).start()
    fill_matrices(k_ref, e_ref, k3_ref, k0_ref, e3_ref)
    early_steps(held_ref, ROWS, (cos_ref, sin_ref), middle, target, k3_ref, k0_ref, lambda i: incoming(i).wait())


def late_kernel(x1, *refs):
    source, (k3_ref, e3_ref), tables, (own_ref, send_ref) = refs[:4], refs[4:6], refs[6:8], refs[8:10]
    states = (refs[10:14], refs[14:18])

    def done(merged, n, step, box, direction, flip):
        return finish(merged, n, step, insert_bit(box, 3, x1), direction, flip, tables)

    for y1 in range(2):
        for half in range(2):
            boxes = [half * 16 + (n // 2 * 4 + y1 * 2 + n % 2) for n in range(SUB)]
            rows = [children(source, insert_bit(box, 3, x1), insert_bit(box, 3, 1 - x1)) for box in boxes]
            merged = product(rows, k3_ref[0, x1, y1])
            for n, box in enumerate(boxes):
                store(states[0], box, *done(merged, n, 2, box, 0, y1))

    def middle(step, bit, after, direction, source, target):
        for h in range(2):
            for flip in range(2):
                if direction == 0:
                    pairs = [[insert_bit(insert_bit(n, after, flip), bit, c) for c in (h, 1 - h)] for n in range(SUB)]
                else:
                    pairs = [[insert_bit(insert_bit(n, bit, c), after, flip) for c in (h, 1 - h)] for n in range(SUB)]
                merged = product([children(source, *pair) for pair in pairs], k3_ref[direction, h, flip])
                for n, (box, _) in enumerate(pairs):
                    store(target, box, *done(merged, n, step, box, direction, flip))

    middle(3, 1, 3, 1, states[0], states[1])
    middle(4, 3, 2, 0, states[1], states[0])
    middle(5, 2, 4, 1, states[0], states[1])
    middle(6, 4, 0, 0, states[1], states[0])

    for quarter in range(2):
        tiles = {}
        for h in range(2):
            boxes = [quarter * 16 + 2 * n for n in range(SUB)]
            merged = product([children(states[0], box + h, box + 1 - h) for box in boxes], k3_ref[1, h, 0])
            for n, box in enumerate(boxes):
                high, low = split_two(jnp.concatenate(done(merged, n, 7, box + h, 1, 0), axis=1))
                tiles[2 * n + h] = jnp.concatenate([high, low, high], axis=1)
        for part in range(2):
            rows = [tiles[8 * part + n // 4 * 4 + (0, 2, 1, 3)[n % 4]] for n in range(8)]
            field = lax.dot_general(
                e3_ref[...], jnp.concatenate(rows, axis=0), (((1,), (1,)), ((), ())), preferred_element_type=F32
            )
            at = 512 * quarter + 256 * part
            own_ref[:, at : at + 256] = field[0:64]
            send_ref[:, at : at + 256] = field[64:128]


VMEM = pl.BlockSpec(memory_space=pltpu.VMEM)
TABLE = jax.ShapeDtypeStruct((32, ROWS, 128), F32)
STATE = jax.ShapeDtypeStruct((64, ROWS, 128), BF16)
FIELD = jax.ShapeDtypeStruct((64, 1024), F32)
K3 = jax.ShapeDtypeStruct((2, 2, 2, 768, 256), BF16)
K0 = pltpu.VMEM((2, 768, 256), BF16)
E3 = jax.ShapeDtypeStruct((128, 768), BF16)


def cost(flops):
    return pl.CostEstimate(flops=flops, bytes_accessed=4 << 20, transcendentals=0)


def first_part(arrived, k, e):
    return pl.pallas_call(
        first_kernel,
        out_shape=[STATE] * 4 + [TABLE] * 4 + [K3, E3],
        in_specs=[VMEM] * 3,
        out_specs=[VMEM] * 10,
        scratch_shapes=[K0] + [pltpu.VMEM(STATE.shape, BF16)] * 4,
        compiler_params=pltpu.CompilerParams(vmem_limit_bytes=MAIN_VMEM),
        cost_estimate=cost(4_000_000_000),
    )(arrived, k, e)


def second_part(arrived, k, e, cos, sin):
    return pl.pallas_call(
        second_kernel,
        out_shape=[STATE] * 4 + [K3, E3],
        in_specs=[pl.BlockSpec(memory_space=pl.ANY)] + [VMEM] * 4,
        out_specs=[VMEM] * 6,
        scratch_shapes=[K0]
        + [pltpu.VMEM(STATE.shape, BF16)] * 4
        + [pltpu.VMEM((128 * ROWS, 128), F32), pltpu.SemaphoreType.DMA((2,))],
        compiler_params=pltpu.CompilerParams(vmem_limit_bytes=MAIN_VMEM),
        cost_estimate=cost(3_000_000_000),
    )(arrived, k, e, cos, sin)


def late_part(x1, state, k3, e3, cos, sin):
    return pl.pallas_call(
        functools.partial(late_kernel, x1),
        out_shape=[FIELD, FIELD],
        in_specs=[VMEM] * 8,
        out_specs=[VMEM] * 2,
        scratch_shapes=[pltpu.VMEM((32, ROWS, 128), BF16)] * 8,
        compiler_params=pltpu.CompilerParams(vmem_limit_bytes=MAIN_VMEM),
        cost_estimate=cost(5_000_000_000),
    )(*state, k3, e3, cos, sin)


def join_kernel(place, w_ref, own_ref, got_ref, *rest):
    out_ref, held_ref, sems = rest[-3:]
    first = w_ref[0] == 0
    lane = lax.broadcasted_iota(jnp.int32, (64, 128), 1)
    even = lane // 32 % 2 == 0
    copies = []
    for box in range(4):
        for y2 in range(2):
            lanes = slice(256 * box + 128 * y2, 256 * box + 128 * y2 + 128)
            own = own_ref[:, lanes]
            got = got_ref[:, lanes]
            a = jnp.where(first, own, got)
            b = jnp.where(first, got, own)
            held_ref[box, :, 256 * y2 : 256 * y2 + 128] = jnp.where(even, a, pltpu.roll(b, 32, 1))
            held_ref[box, :, 256 * y2 + 128 : 256 * y2 + 256] = jnp.where(even, pltpu.roll(a, 96, 1), b)
        at = (4 * box + place) * 512
        copies.append(pltpu.make_async_copy(held_ref.at[box], out_ref.at[:, at : at + 512], sems.at[box]))
        copies[-1].start()
    for copy in copies:
        copy.wait()


def join(w, own, got, place, out):
    more = [] if out is None else [out]
    anywhere = pl.BlockSpec(memory_space=pl.ANY)
    return pl.pallas_call(
        functools.partial(join_kernel, place),
        out_shape=jax.ShapeDtypeStruct((64, 8192), F32),
        in_specs=[pl.BlockSpec(memory_space=pltpu.SMEM), VMEM, VMEM] + [anywhere] * len(more),
        out_specs=anywhere,
        scratch_shapes=[pltpu.VMEM((4, 64, 512), F32), pltpu.SemaphoreType.DMA((4,))],
        input_output_aliases={3: 0} if more else {},
        compiler_params=pltpu.CompilerParams(vmem_limit_bytes=MAIN_VMEM),
        cost_estimate=pl.CostEstimate(flops=0, bytes_accessed=1 << 20, transcendentals=0),
    )(w, own, got, *more)


def merge_matrices(interp_matrix):
    re = jnp.transpose(interp_matrix[:, 0], (0, 3, 4, 1, 2)).reshape(2, 2, 64, 128)
    im = jnp.transpose(interp_matrix[:, 1], (0, 3, 4, 1, 2)).reshape(2, 2, 64, 128)
    from_re = jnp.concatenate([re, im], axis=3)
    from_im = jnp.concatenate([-im, re], axis=3)
    return jnp.stack([from_re, from_im], axis=2).reshape(2, 256, 256)


def evaluation_matrix(evaluation, w):
    zero = jnp.zeros((64, 64), F32)
    re, im = evaluation[0], -evaluation[1]
    low = jnp.concatenate([re, zero, im, zero], axis=1)
    high = jnp.concatenate([zero, re, zero, im], axis=1)
    return jnp.where(w == 0, jnp.concatenate([low, high], axis=0), jnp.concatenate([high, low], axis=0))


def shards(weights, phase_slope, interp_matrix, evaluation):
    w = lax.axis_index("bx") >> 3
    w_one = w.astype(jnp.int32).reshape(1)
    planes = weights.reshape(128, 8192)
    k = merge_matrices(interp_matrix)
    e = evaluation_matrix(evaluation, w)

    def spread(packed):
        return lax.all_to_all(packed.reshape(128, 1, -1), AXES, split_axis=0, concat_axis=0, tiled=True).reshape(-1, 128)

    def swap(field):
        return lax.ppermute(field, "bx", [(i, i ^ 8) for i in range(16)])

    arrived0 = spread(pack(planes, phase_slope.reshape(8, 1, 8192), 0))
    arrived1 = spread(pack(planes, None, 1))
    *first, cos0, sin0, cos1, sin1, k3, e3 = first_part(arrived0, k, e)
    fields = [late_part(x1, first, k3, e3, cos0, sin0) for x1 in range(2)]
    *second, k3, e3 = second_part(arrived1, k, e, cos1, sin1)
    fields += [late_part(x1, second, k3, e3, cos1, sin1) for x1 in range(2)]
    out = None
    for n, (own, send) in enumerate(fields):
        out = join(w_one, own, swap(send), n % 2 * 2 + n // 2, out)
    return out[None, None]


def solution(mesh):
    in_specs = (P("bx", "by", None, None, None), P(None, "bx", "by", None), P(), P())
    out_specs = P("bx", "by", None, None)
    return jax.shard_map(shards, mesh=mesh, in_specs=in_specs, out_specs=out_specs, check_vma=False)
```

```python
import functools

import jax
import jax.numpy as jnp
import numpy as np
from jax import lax
from jax.experimental import pallas as pl
from jax.experimental.pallas import tpu as pltpu
from jax.sharding import PartitionSpec as P

PACK_VMEM = 60 << 20
MAIN_VMEM = 24 << 20
AXES = ("bx", "by")
ROWS = 32
SLOPES = 4
NODES = [float(np.cos(np.pi * (2 * m + 1) / 16)) for m in range(4)]
F32 = jnp.float32
BF16 = jnp.bfloat16


def split_two(value):
    high = value.astype(BF16)
    low = (value - high.astype(F32)).astype(BF16)
    return high, low


def pack_kernel(top, rows, w_ref, *refs):
    p_ref = refs[0] if rows > ROWS else None
    out_ref, held_ref, made_ref, p_held_ref, in_sems, out_sems = refs[-6:]
    pieces, _, lanes = held_ref.shape
    half = pieces * lanes
    tall = lanes // 64 * rows

    def incoming(n):
        at = pl.ds(pl.multiple_of(top * half + n * lanes, 128), lanes)
        return pltpu.make_async_copy(w_ref.at[:, at], held_ref.at[n], in_sems.at[n])

    def outgoing(n, w):
        at = pl.ds(pl.multiple_of(n * tall, 8), tall)
        return pltpu.make_async_copy(made_ref.at[w, at], out_ref.at[w, at], out_sems.at[n, w])

    more = []
    if p_ref is not None:
        more = [pltpu.make_async_copy(p_ref, p_held_ref, in_sems.at[pieces])]
        more[0].start()
    for n in range(pieces):
        incoming(n).start()
    if p_ref is not None:
        more[0].wait()

        @pl.loop(0, pieces)
        def _(n):
            first = pl.multiple_of(n * tall, 8)
            p0 = p_held_ref[:, 0, pl.ds(pl.multiple_of(n * lanes, 128), lanes)]
            p1 = p_held_ref[:, 0, pl.ds(pl.multiple_of(half + n * lanes, 128), lanes)]
            for b in range(lanes // 64):
                for w in range(2):
                    at = slice(64 * b + 32 * w, 64 * b + 32 * w + 32)
                    parts = [p0[0:4, at], p1[0:4, at], p0[4:8, at], p1[4:8, at]]
                    to = first + (b * rows + ROWS)
                    made_ref[w, pl.ds(to, SLOPES), :] = jnp.concatenate(parts, axis=1)

    @pl.loop(0, pieces)
    def _(n):
        incoming(n).wait()
        first = pl.multiple_of(n * tall, 8)
        for pair in range(lanes // 128):
            turned = held_ref[n, :, pair * 128 : pair * 128 + 128].T
            for b in range(2):
                for w in range(2):
                    at = 64 * b + 32 * w
                    made_ref[w, pl.ds(first + (2 * pair + b) * rows, ROWS), :] = turned[at : at + 32]
        for w in range(2):
            outgoing(n, w).start()

    @pl.loop(0, pieces)
    def _(n):
        for w in range(2):
            outgoing(n, w).wait()


def pack(weights, slopes, top):
    pieces, lanes = 2, 2048
    rows = ROWS if slopes is None else ROWS + SLOPES
    more = [] if slopes is None else [slopes]
    anywhere = pl.BlockSpec(memory_space=pl.ANY)
    return pl.pallas_call(
        functools.partial(pack_kernel, top, rows),
        out_shape=jax.ShapeDtypeStruct((2, 64 * rows, 128), F32),
        in_specs=[anywhere] * (1 + len(more)),
        out_specs=anywhere,
        scratch_shapes=[
            pltpu.VMEM((pieces, 128, lanes), F32),
            pltpu.VMEM((2, 64 * rows, 128), F32),
            pltpu.VMEM((8, 1, 8192), F32),
            pltpu.SemaphoreType.DMA((pieces + 1,)),
            pltpu.SemaphoreType.DMA((pieces, 2)),
        ],
        compiler_params=pltpu.CompilerParams(vmem_limit_bytes=PACK_VMEM),
        cost_estimate=pl.CostEstimate(flops=0, bytes_accessed=5 << 20, transcendentals=0),
    )(weights, *more)


def sincos(angle):
    h = angle * 0.5
    q = h * h
    s = q * (-1 / 39916800) + 1 / 362880
    s = s * q - 1 / 5040
    s = s * q + 1 / 120
    s = s * q - 1 / 6
    s = (s * q + 1.0) * h
    c = q * (1 / 479001600) - 1 / 3628800
    c = c * q + 1 / 40320
    c = c * q - 1 / 720
    c = c * q + 1 / 24
    c = c * q - 0.5
    c = c * q + 1.0
    return 2.0 * s * c, 1.0 - 2.0 * s * s


def lane_gather(value, index):
    return jnp.take_along_axis(value, index, axis=1, mode="promise_in_bounds")


def build_tables(a_ref, tables):
    lane = lax.broadcasted_iota(jnp.int32, (ROWS, 128), 1)
    m = lane % 4
    node = jnp.where(m == 0, NODES[0], jnp.where(m == 1, NODES[1], jnp.where(m == 2, NODES[2], NODES[3])))
    second = lane // 4 % 2 == 1
    g = lane // 8

    @pl.loop(0, SLOPES)
    def _(row):
        turned = a_ref[pl.ds(ROWS + row, 128, stride=ROWS + SLOPES), :].T
        for late in range(2):
            t0 = turned[64 * late : 64 * late + 32]
            t1 = turned[64 * late + 32 : 64 * late + 64]
            for tile in range(4):
                for h, (cos_ref, sin_ref) in enumerate(tables):
                    index = ((2 * (2 * tile + g // 8) + h) * 8) + g % 8
                    slope = jnp.where(second, lane_gather(t1, index), lane_gather(t0, index))
                    s, c = sincos(slope * node)
                    at = (row + SLOPES * late) * 4 + tile
                    cos_ref[at] = c
                    sin_ref[at] = s


def factors(step, box, direction, flip, cos_ref, sin_ref):
    lane = lax.broadcasted_iota(jnp.int32, (ROWS, 128), 1)
    p = lane % 64
    m = p // 8 if direction == 0 else p % 8
    index = (lane // 64 + flip) % 2 * 4 + jnp.where(m < 4, m, 7 - m) + (box % 16) * 8
    tile = step * 4 + box // 16
    c = lane_gather(cos_ref[tile], index)
    s = lane_gather(sin_ref[tile], index)
    return c, jnp.where(m < 4, s, -s)


def rotate(merged, c, s):
    re = merged[:, :128]
    im = merged[:, 128:]
    return re * c - im * s, re * s + im * c


def insert_bit(q, bit, value):
    return ((q >> bit) << (bit + 1)) | (value << bit) | (q & ((1 << bit) - 1))


SUB = 8


def fill_matrices(k_ref, e_ref, k3_ref, k0_ref, e3_ref):
    def fill(to, value):
        high, low = split_two(value)
        to[0:256] = high
        to[256:512] = high
        to[512:768] = low

    for d in range(2):
        for flip in range(2):
            value = k_ref[d]
            if flip:
                value = jnp.concatenate([pltpu.roll(value[:, 128 * n : 128 * n + 128], 64, 1) for n in range(2)], axis=1)
            if d == 0:
                fill(k0_ref.at[flip], value)
            for h in range(2):
                parts = [value[128 * c + 64 * part : 128 * c + 64 * part + 64] for part in range(2) for c in (h, 1 - h)]
                fill(k3_ref.at[d, h, flip], jnp.concatenate(parts, axis=0))
    high, low = split_two(e_ref[...])
    e3_ref[:, 0:256] = high
    e3_ref[:, 256:512] = high
    e3_ref[:, 512:768] = low


def product(rows, matrix):
    return jnp.dot(jnp.concatenate(rows, axis=0), matrix, preferred_element_type=F32)


def children(state, first, second):
    lower = lax.broadcasted_iota(jnp.int32, (ROWS, 128), 1).astype(F32).astype(BF16) < 64
    high_re, high_im, low_re, low_im = (jnp.where(lower, ref[first], ref[second]) for ref in state)
    return jnp.concatenate([high_re, high_im, low_re, low_im, high_re, high_im], axis=1)


def store(state, box, re, im):
    state[0][box], state[2][box] = split_two(re)
    state[1][box], state[3][box] = split_two(im)


def finish(merged, n, step, box, direction, flip, tables):
    c, s = factors(step, box, direction, flip, *tables)
    return rotate(merged[ROWS * n : ROWS * n + ROWS], c, s)


def early_steps(a_ref, stride, tables, middle, target, k3_ref, k0_ref, ready=lambda i: None):
    def arrived(pair, odd):
        at = (2 * pair + odd) * stride
        return a_ref[at : at + ROWS, :]

    for i in range(2):
        ready(i)
        for sub in range(0, 32, 2 * SUB):
            for y0 in range(2):
                boxes = [i * 32 + (sub + 2 * n + y0) for n in range(SUB)]
                rows = []
                for n in range(SUB):
                    pair = i * 32 + (sub // 8 * 8 + n // 4 * 8 + n % 4)
                    parts = [split_two(arrived(pair + 4 * c, y0)) for c in range(2)]
                    highs = [p[0] for p in parts]
                    lows = [p[1] for p in parts]
                    rows.append(jnp.concatenate(highs + lows + highs, axis=1))
                merged = product(rows, k0_ref[y0])
                for n, box in enumerate(boxes):
                    store(middle, box, *finish(merged, n, 0, box, 0, y0, tables))

    for i in range(2):
        for h in range(2):
            for x1 in range(2):
                pairs = [i * 32 + (n // 4 * 16 + x1 * 8 + n % 4 * 2) for n in range(SUB)]
                merged = product([children(middle, q + h, q + 1 - h) for q in pairs], k3_ref[1, h, x1])
                for n in range(SUB):
                    store(target, pairs[n] + h, *finish(merged, n, 1, pairs[n] + h, 1, x1, tables))


def first_kernel(a_ref, k_ref, e_ref, *refs):
    target, tables, (k3_ref, e3_ref, k0_ref), middle = refs[:4], refs[4:8], refs[8:11], refs[11:]
    build_tables(a_ref, (tables[:2], tables[2:]))
    fill_matrices(k_ref, e_ref, k3_ref, k0_ref, e3_ref)
    early_steps(a_ref, ROWS + SLOPES, tables[:2], middle, target, k3_ref, k0_ref)


def second_kernel(a_ref, k_ref, e_ref, cos_ref, sin_ref, *refs):
    target, (k3_ref, e3_ref, k0_ref), middle, (held_ref, sems) = refs[:4], refs[4:7], refs[7:11], refs[11:]

    def incoming(i):
        rows = pl.ds(pl.multiple_of(i * 64 * ROWS, 8), 64 * ROWS)
        return pltpu.make_async_copy(a_ref.at[rows], held_ref.at[rows], sems.at[i])

    for i in range(2):
        incoming(i).start()
    fill_matrices(k_ref, e_ref, k3_ref, k0_ref, e3_ref)
    early_steps(held_ref, ROWS, (cos_ref, sin_ref), middle, target, k3_ref, k0_ref, lambda i: incoming(i).wait())


def late_kernel(x1, *refs):
    source, (k3_ref, e3_ref), tables, (own_ref, send_ref) = refs[:4], refs[4:6], refs[6:8], refs[8:10]
    states = (refs[10:14], refs[14:18])

    def done(merged, n, step, box, direction, flip):
        return finish(merged, n, step, insert_bit(box, 3, x1), direction, flip, tables)

    for y1 in range(2):
        for half in range(2):
            boxes = [half * 16 + (n // 2 * 4 + y1 * 2 + n % 2) for n in range(SUB)]
            rows = [children(source, insert_bit(box, 3, x1), insert_bit(box, 3, 1 - x1)) for box in boxes]
            merged = product(rows, k3_ref[0, x1, y1])
            for n, box in enumerate(boxes):
                store(states[0], box, *done(merged, n, 2, box, 0, y1))

    def middle(step, bit, after, direction, source, target):
        for h in range(2):
            for flip in range(2):
                if direction == 0:
                    pairs = [[insert_bit(insert_bit(n, after, flip), bit, c) for c in (h, 1 - h)] for n in range(SUB)]
                else:
                    pairs = [[insert_bit(insert_bit(n, bit, c), after, flip) for c in (h, 1 - h)] for n in range(SUB)]
                merged = product([children(source, *pair) for pair in pairs], k3_ref[direction, h, flip])
                for n, (box, _) in enumerate(pairs):
                    store(target, box, *done(merged, n, step, box, direction, flip))

    middle(3, 1, 3, 1, states[0], states[1])
    middle(4, 3, 2, 0, states[1], states[0])
    middle(5, 2, 4, 1, states[0], states[1])
    middle(6, 4, 0, 0, states[1], states[0])

    for quarter in range(2):
        tiles = {}
        for h in range(2):
            boxes = [quarter * 16 + 2 * n for n in range(SUB)]
            merged = product([children(states[0], box + h, box + 1 - h) for box in boxes], k3_ref[1, h, 0])
            for n, box in enumerate(boxes):
                high, low = split_two(jnp.concatenate(done(merged, n, 7, box + h, 1, 0), axis=1))
                tiles[2 * n + h] = jnp.concatenate([high, low, high], axis=1)
        for part in range(2):
            rows = [tiles[8 * part + n // 4 * 4 + (0, 2, 1, 3)[n % 4]] for n in range(8)]
            field = lax.dot_general(
                e3_ref[...], jnp.concatenate(rows, axis=0), (((1,), (1,)), ((), ())), preferred_element_type=F32
            )
            at = 512 * quarter + 256 * part
            own_ref[:, at : at + 256] = field[0:64]
            send_ref[:, at : at + 256] = field[64:128]


VMEM = pl.BlockSpec(memory_space=pltpu.VMEM)
TABLE = jax.ShapeDtypeStruct((32, ROWS, 128), F32)
STATE = jax.ShapeDtypeStruct((64, ROWS, 128), BF16)
FIELD = jax.ShapeDtypeStruct((64, 1024), F32)
K3 = jax.ShapeDtypeStruct((2, 2, 2, 768, 256), BF16)
K0 = pltpu.VMEM((2, 768, 256), BF16)
E3 = jax.ShapeDtypeStruct((128, 768), BF16)


def cost(flops):
    return pl.CostEstimate(flops=flops, bytes_accessed=4 << 20, transcendentals=0)


def first_part(arrived, k, e):
    return pl.pallas_call(
        first_kernel,
        out_shape=[STATE] * 4 + [TABLE] * 4 + [K3, E3],
        in_specs=[VMEM] * 3,
        out_specs=[VMEM] * 10,
        scratch_shapes=[K0] + [pltpu.VMEM(STATE.shape, BF16)] * 4,
        compiler_params=pltpu.CompilerParams(vmem_limit_bytes=MAIN_VMEM),
        cost_estimate=cost(4_000_000_000),
    )(arrived, k, e)


def second_part(arrived, k, e, cos, sin):
    return pl.pallas_call(
        second_kernel,
        out_shape=[STATE] * 4 + [K3, E3],
        in_specs=[pl.BlockSpec(memory_space=pl.ANY)] + [VMEM] * 4,
        out_specs=[VMEM] * 6,
        scratch_shapes=[K0]
        + [pltpu.VMEM(STATE.shape, BF16)] * 4
        + [pltpu.VMEM((128 * ROWS, 128), F32), pltpu.SemaphoreType.DMA((2,))],
        compiler_params=pltpu.CompilerParams(vmem_limit_bytes=MAIN_VMEM),
        cost_estimate=cost(3_000_000_000),
    )(arrived, k, e, cos, sin)


def late_part(x1, state, k3, e3, cos, sin):
    return pl.pallas_call(
        functools.partial(late_kernel, x1),
        out_shape=[FIELD, FIELD],
        in_specs=[VMEM] * 8,
        out_specs=[VMEM] * 2,
        scratch_shapes=[pltpu.VMEM((32, ROWS, 128), BF16)] * 8,
        compiler_params=pltpu.CompilerParams(vmem_limit_bytes=MAIN_VMEM),
        cost_estimate=cost(5_000_000_000),
    )(*state, k3, e3, cos, sin)


def join_kernel(place, w_ref, own_ref, got_ref, *rest):
    out_ref, held_ref, sems = rest[-3:]
    first = w_ref[0] == 0
    lane = lax.broadcasted_iota(jnp.int32, (64, 128), 1)
    even = lane // 32 % 2 == 0
    copies = []
    for box in range(4):
        for y2 in range(2):
            lanes = slice(256 * box + 128 * y2, 256 * box + 128 * y2 + 128)
            own = own_ref[:, lanes]
            got = got_ref[:, lanes]
            a = jnp.where(first, own, got)
            b = jnp.where(first, got, own)
            held_ref[box, :, 256 * y2 : 256 * y2 + 128] = jnp.where(even, a, pltpu.roll(b, 32, 1))
            held_ref[box, :, 256 * y2 + 128 : 256 * y2 + 256] = jnp.where(even, pltpu.roll(a, 96, 1), b)
        at = (4 * box + place) * 512
        copies.append(pltpu.make_async_copy(held_ref.at[box], out_ref.at[:, at : at + 512], sems.at[box]))
        copies[-1].start()
    for copy in copies:
        copy.wait()


def join(w, own, got, place, out):
    more = [] if out is None else [out]
    anywhere = pl.BlockSpec(memory_space=pl.ANY)
    return pl.pallas_call(
        functools.partial(join_kernel, place),
        out_shape=jax.ShapeDtypeStruct((64, 8192), F32),
        in_specs=[pl.BlockSpec(memory_space=pltpu.SMEM), VMEM, VMEM] + [anywhere] * len(more),
        out_specs=anywhere,
        scratch_shapes=[pltpu.VMEM((4, 64, 512), F32), pltpu.SemaphoreType.DMA((4,))],
        input_output_aliases={3: 0} if more else {},
        compiler_params=pltpu.CompilerParams(vmem_limit_bytes=MAIN_VMEM),
        cost_estimate=pl.CostEstimate(flops=0, bytes_accessed=1 << 20, transcendentals=0),
    )(w, own, got, *more)


def merge_matrices(interp_matrix):
    re = jnp.transpose(interp_matrix[:, 0], (0, 3, 4, 1, 2)).reshape(2, 2, 64, 128)
    im = jnp.transpose(interp_matrix[:, 1], (0, 3, 4, 1, 2)).reshape(2, 2, 64, 128)
    from_re = jnp.concatenate([re, im], axis=3)
    from_im = jnp.concatenate([-im, re], axis=3)
    return jnp.stack([from_re, from_im], axis=2).reshape(2, 256, 256)


def evaluation_matrix(evaluation, w):
    zero = jnp.zeros((64, 64), F32)
    re, im = evaluation[0], -evaluation[1]
    low = jnp.concatenate([re, zero, im, zero], axis=1)
    high = jnp.concatenate([zero, re, zero, im], axis=1)
    return jnp.where(w == 0, jnp.concatenate([low, high], axis=0), jnp.concatenate([high, low], axis=0))


def shards(weights, phase_slope, interp_matrix, evaluation):
    w = lax.axis_index("bx") >> 3
    w_one = w.astype(jnp.int32).reshape(1)
    planes = weights.reshape(128, 8192)
    k = merge_matrices(interp_matrix)
    e = evaluation_matrix(evaluation, w)

    def spread(packed):
        return lax.all_to_all(packed.reshape(128, 1, -1), AXES, split_axis=0, concat_axis=0, tiled=True).reshape(-1, 128)

    def swap(field):
        return lax.ppermute(field, "bx", [(i, i ^ 8) for i in range(16)])

    arrived0 = spread(pack(planes, phase_slope.reshape(8, 1, 8192), 0))
    arrived1 = spread(pack(planes, None, 1))
    *first, cos0, sin0, cos1, sin1, k3, e3 = first_part(arrived0, k, e)
    fields = [late_part(x1, first, k3, e3, cos0, sin0) for x1 in range(2)]
    *second, k3, e3 = second_part(arrived1, k, e, cos1, sin1)
    fields += [late_part(x1, second, k3, e3, cos1, sin1) for x1 in range(2)]
    out = None
    for n, (own, send) in enumerate(fields):
        out = join(w_one, own, swap(send), n % 2 * 2 + n // 2, out)
    return out[None, None]


def solution(mesh):
    in_specs = (P("bx", "by", None, None, None), P(None, "bx", "by", None), P(), P())
    out_specs = P("bx", "by", None, None)
    return jax.shard_map(shards, mesh=mesh, in_specs=in_specs, out_specs=out_specs, check_vma=False)
```
